512 devices in a mesh: rows: 32 (over z, x_hi, core), rep: 16 (over x_lo, y).
Axes of the slice: x: 4 (x_hi: 2, x_lo: 2; x = x_hi * 2 + x_lo), y: 8, z: 8, core: 2. Of those that a mesh axis runs over, the one named last changes fastest.
Arguments:
- features: bfloat16 [65536, 256], P(('rows', 'rep')), may hold values from -6 to 6
- adjacency: bfloat16 [32, 32, 16, 128, 128], P('rows', 'rep'), may hold values from -0.09375 to 0.09375
- tile_ids: int32 [32, 32, 16], P('rows', 'rep'), may hold values from 0 to 255, as said below
- tile_counts: int32 [32, 32], P('rows', 'rep'), may hold values from 1 to 16, as said below
- weight: bfloat16 [256, 256], replicated, may hold values from -0.375 to 0.375
- grad_out: bfloat16 [65536, 256], P(('rows', 'rep')), may hold values from -6 to 6
Outputs:
- activated: bfloat16 [65536, 256], P(('rows', 'rep'))
- grad_weight: float32 [256, 256], P(None, 'rep')
- grad_features: float32 [32, 2048, 256], P('rep', 'rows')
The draws below stay inside these ranges and needn't reach their ends.
Inputs may be any that keep to these rules, and one draw needn't show every extreme that they name: `tile_ids`: within one row block and section the 16 entries are distinct; an entry v names tile row v // 16 and tile column v % 16. Only the first tile_counts[r, s] slots of a row block and section hold tiles of the matrix; later slots are padding.
All inputs are finite; a program needn't handle non-finite values.
Results may differ from the reference program's by a relative error of at most 0.025.
Values may be sent and summed in bfloat16 or wider, within the bound.
A program may use at most 64 MiB of HBM per device.

```python
import jax
import jax.numpy as jnp
from jax import lax

F = 256
H = 256
TILE = 128
TPB = 16
SLOTS = 16
NR = 2048
NODES = 65536
SECTION_DEV = 2
N_ROWS = 32
N_REP = 16


def draw_tile_ids(key, part):
    key = jax.random.fold_in(key, 11)
    many_keys = jax.random.split(key, N_ROWS * N_ROWS)
    chosen = jax.vmap(lambda one_key: jax.random.permutation(one_key, TPB * TPB)[:SLOTS])(many_keys)
    return chosen.reshape(N_ROWS, N_ROWS, SLOTS).astype(jnp.int32)


def draw_tile_counts(key, part):
    key = jax.random.fold_in(key, 23)
    first_key, second_key, heavy_key, place_key = jax.random.split(key, 4)
    first = jax.random.randint(first_key, (N_ROWS, N_ROWS), 1, SLOTS + 1)
    second = jax.random.randint(second_key, (N_ROWS, N_ROWS), 1, SLOTS + 1)
    heavy = jax.random.randint(heavy_key, (N_ROWS, N_ROWS), 0, 4) == 0
    counts = jnp.where(heavy, SLOTS, jnp.minimum(first, second))
    position = jax.random.randint(place_key, (), 0, N_ROWS * N_ROWS)
    counts = counts.reshape(N_ROWS * N_ROWS).at[position].set(SLOTS)
    return counts.reshape(N_ROWS, N_ROWS).astype(jnp.int32)


def spiked(drawn, own_key, source, target, blocks, factor):
    owner, partner = [(jnp.arange(drawn.shape[dim]) // (drawn.shape[dim] // blocks)).reshape([-1 if axis == dim else 1 for axis in range(drawn.ndim)]) for dim in (source, target)]
    chosen = jax.random.permutation(own_key, blocks)[partner]
    strong = (owner == chosen) | (owner == (partner + blocks // 2) % blocks)
    return jnp.where(strong, factor * drawn, drawn)


def levels(key, dims, pieces, smallest, top_value):
    level = 1.0
    for dim, blocks in pieces:
        heights = jax.random.uniform(jax.random.fold_in(jax.random.fold_in(key, 6), dim), (blocks,), jnp.float32, smallest / len(pieces), top_value / len(pieces))
        level = level * jnp.repeat(jnp.exp(heights), dims[dim] // blocks).reshape((-1,) + (1,) * (len(dims) - 1 - dim))
    return level


def normal_values(rng, dims, spread, reach, cuts=(), held_as=jnp.bfloat16):
    drawn = jax.random.normal(rng, dims, jnp.float32) * spread
    if len(cuts) > 0:
        drawn = levels(rng, dims, cuts, -0.22, 0.18) * drawn
    return jnp.clip(drawn, min=-reach, max=reach).astype(held_as)


def bell_draw_with(own_key, extent, spread, limit, cuts, heavy, kind=jnp.bfloat16):
    array = spread * jax.random.normal(own_key, extent, jnp.float32)
    if cuts:
        array = array * levels(own_key, extent, cuts, -0.22, 0.18)
    return jnp.clip(spiked(array, jax.random.fold_in(own_key, 3), *heavy), -limit, limit).astype(kind)


def setup_inputs(seed: int = 0) -> dict:
    key_list = jax.random.split(jax.random.key(seed), 7)
    features = normal_values(key_list[0], (NODES, F), 1.0, 6.0, ((0, 512),))
    adjacency = normal_values(key_list[1], (N_ROWS, N_ROWS, SLOTS, TILE, TILE), (N_ROWS * SLOTS * TILE // TPB) ** -0.5, 0.09375, ((0, 32), (1, 16)))
    tile_ids = draw_tile_ids(jax.random.fold_in(key_list[6], 71), 0)
    tile_counts = draw_tile_counts(jax.random.fold_in(key_list[6], 71), 0)
    weight = normal_values(key_list[4], (F, H), F ** -0.5, 0.375)
    grad_out = bell_draw_with(key_list[5], (NODES, H), 0.25, 6.0, ((0, 512),), (0, 1, 256, 6.0))
    return dict(features=features, adjacency=adjacency, tile_ids=tile_ids, tile_counts=tile_counts, weight=weight, grad_out=grad_out)


def place_rows(product, slot_ids, tile_count, target, tiles_per):
    live_mask = (jnp.arange(slot_ids.shape[0], dtype=jnp.int32) < tile_count).astype(product.dtype)
    masked = product * live_mask[:, None, None]
    placed = jnp.zeros((tiles_per, product.shape[1], product.shape[2]), product.dtype).at[target].add(masked)
    return placed.reshape(tiles_per * product.shape[1], product.shape[2])


def forward_tiles(tile_block, slot_ids, tile_count, section_rows):
    tile_size = tile_block.shape[-1]
    tiles_per = section_rows.shape[0] // tile_size
    row_tile = slot_ids // tiles_per
    col_tile = slot_ids % tiles_per
    blocked = section_rows.reshape(tiles_per, tile_size, section_rows.shape[1])
    picked = jnp.take(blocked, col_tile, axis=0)
    product = jnp.einsum("tij,tjf->tif", tile_block.astype(jnp.float32), picked.astype(jnp.float32))
    return place_rows(product, slot_ids, tile_count, row_tile, tiles_per)


def backward_tiles(tile_block, slot_ids, tile_count, block_grad):
    tile_size = tile_block.shape[-1]
    tiles_per = block_grad.shape[0] // tile_size
    row_tile = slot_ids // tiles_per
    col_tile = slot_ids % tiles_per
    blocked = block_grad.reshape(tiles_per, tile_size, block_grad.shape[1])
    picked = jnp.take(blocked, row_tile, axis=0)
    product = jnp.einsum("tji,tjf->tif", tile_block.astype(jnp.float32), picked.astype(jnp.float32))
    return place_rows(product, slot_ids, tile_count, col_tile, tiles_per)


def reference(features, adjacency, tile_ids, tile_counts, weight, grad_out):
    blocks = features.reshape(N_ROWS, NR, F)

    def row_block(row_index):
        section_terms = jax.vmap(forward_tiles)(adjacency[row_index], tile_ids[row_index], tile_counts[row_index], blocks)
        grouped = section_terms.reshape(N_REP, SECTION_DEV, NR, F).sum(axis=1).astype(jnp.bfloat16)
        grouped = lax.optimization_barrier(grouped).astype(jnp.float32)
        return grouped.sum(axis=0).astype(jnp.bfloat16)

    aggregated = lax.map(row_block, jnp.arange(N_ROWS, dtype=jnp.int32)).reshape(NODES, F)
    pre_act = jnp.dot(aggregated, weight, preferred_element_type=jnp.float32)
    gate_value = jax.nn.sigmoid(pre_act)
    activated = (pre_act * gate_value).astype(jnp.bfloat16)
    grad_pre = (grad_out.astype(jnp.float32) * gate_value * (1.0 + pre_act * (1.0 - gate_value))).astype(jnp.bfloat16)
    grad_weight = jnp.dot(aggregated.T, grad_pre, preferred_element_type=jnp.float32)
    grad_agg = jnp.dot(grad_pre, weight.T, preferred_element_type=jnp.float32).astype(jnp.bfloat16).reshape(N_ROWS, NR, F)

    def column_block(section_num):
        section_terms = jax.vmap(backward_tiles)(adjacency[:, section_num], tile_ids[:, section_num], tile_counts[:, section_num], grad_agg)
        rounded = lax.optimization_barrier(section_terms.astype(jnp.bfloat16)).astype(jnp.float32)
        return rounded.sum(axis=0)

    grad_features = lax.map(column_block, jnp.arange(N_ROWS, dtype=jnp.int32))
    return activated, grad_weight, grad_features
```

```python
import functools

import jax
import jax.numpy as jnp
from jax import lax
from jax.experimental import pallas as pl
from jax.experimental.pallas import tpu as pltpu
from jax.sharding import PartitionSpec as P

N = 8
Q = 2 * N
HALF = N // 2
TILE = 128
SLOTS = 16
NT = 2 * SLOTS
SHIFT = N
F32 = jnp.float32
BF16 = jnp.bfloat16
MESH = pl.DeviceIdType.MESH
N_SEMS = 192


class Links:
    def __init__(self, send_sems, recv_sems):
        self.send_sems, self.recv_sems, self.copies = send_sems, recv_sems, []

    def send(self, src, dst, device):
        i = len(self.copies)
        copy = pltpu.make_async_remote_copy(
            src_ref=src,
            dst_ref=dst,
            send_sem=self.send_sems.at[i],
            recv_sem=self.recv_sems.at[i],
            device_id=device,
            device_id_type=MESH,
        )
        copy.start()
        self.copies.append(copy)
        return copy

    def finish(self):
        for copy in self.copies:
            copy.wait_send()


def wait(copies):
    for copy in copies:
        copy.wait_recv()


def gather_ring(links, buf, pos, sub, right, left, partner, arrived=None):
    own, other = buf.at[pos * 2 + sub], buf.at[pos * 2 + 1 - sub]
    pair = links.send(own, own, partner)
    to_right, to_left = [links.send(own, own, right)], [links.send(own, own, left)]
    yield
    pair.wait_recv()
    to_right.append(links.send(other, other, right))
    to_left.append(links.send(other, other, left))
    if arrived:
        arrived(pos)
    yield
    for k in range(1, HALF):
        rp, lp = lax.rem(pos + N - k, N), lax.rem(pos + k, N)
        last = k == HALF - 1
        wait(to_right)
        chunk = buf.at[pl.ds(rp * 2, 1 if last else 2)]
        to_right = [links.send(chunk, chunk, right)]
        if arrived:
            arrived(rp)
        wait(to_left)
        chunk = buf.at[pl.ds(lp * 2 + 1, 1) if last else pl.ds(lp * 2, 2)]
        to_left = [links.send(chunk, chunk, left)]
        if arrived:
            arrived(lp)
        yield
    wait(to_right)
    wait(to_left)
    if arrived:
        arrived(lax.rem(pos + HALF, N))
    yield


def scatter_ring(links, own, prep, from_left, from_right, kept, pair_out, pair_in, pos, sub, right, left, partner, done):
    def add(slot, block):
        return (slot.astype(F32) + block.astype(F32)).astype(BF16)

    far = lax.rem(pos + HALF, N)
    prep(far)
    to_right = links.send(own.at[far * 2], from_left.at[0, 0], right)
    to_left = links.send(own.at[far * 2 + 1], from_right.at[0, 1], left)
    yield
    for k in range(1, HALF):
        rp, lp = lax.rem(pos + HALF - k, N), lax.rem(pos + N - HALF + k, N)
        for arriving, p, slots, device, first in (
            (to_right, rp, from_left, right, 0),
            (to_left, lp, from_right, left, 1),
        ):
            prep(p)
            arriving.wait_recv()
            if k == 1:
                slots[0, first] = add(slots[0, first], own[p * 2 + first])
                slots[0, 1 - first] = own[p * 2 + 1 - first]
            else:
                slots[k - 1, 0] = add(slots[k - 1, 0], own[p * 2])
                slots[k - 1, 1] = add(slots[k - 1, 1], own[p * 2 + 1])
            copy = links.send(slots.at[k - 1], slots.at[k], device)
            if device is right:
                to_right = copy
            else:
                to_left = copy
        yield
    prep(pos)
    wait([to_right, to_left])

    def total(s):
        value = own[pos * 2 + s].astype(F32)
        return value + from_left[HALF - 1, s].astype(F32) + from_right[HALF - 1, s].astype(F32)

    pair_out[...] = total(1 - sub).astype(BF16)
    pair = links.send(pair_out, pair_in, partner)
    kept[...] = total(sub)
    yield
    pair.wait_recv()
    done(kept[...] + pair_in[...].astype(F32))
    yield


def drain(*parts):
    parts = list(parts)
    while parts:
        for part in list(parts):
            if next(part, "end") == "end":
                parts.remove(part)


def step(part, count=1):
    for _ in range(count):
        next(part, None)


def kernel(
    feat, adj, ids, counts, weight, gout,
    act_out, gw_out, gf_out,
    fbuf0, fbuf1, gbuf0, gbuf1, part0, part1, term0, term1, xterm0, xterm1, adj_t, prod, agg, gpre,
    fl0, fr0, fl1, fr1, bl0, br0, bl1, br1, kept, pairs, kept_b, pairs_b,
    wt, wl, wr, wkept, wpair, wsum, wgather,
    kf, kb, pf, pb, lf, lb, send_sems, recv_sems,
):
    row, rep = lax.axis_index("rows"), lax.axis_index("rep")
    z, xh, core = row // 4, lax.rem(row // 2, 2), lax.rem(row, 2)
    xl, y = rep // N, lax.rem(rep, N)
    place = z * 2 + xh

    def device(z=z, xh=xh, core=core, xl=xl, y=y):
        return {"rows": (z * 2 + xh) * 2 + core, "rep": xl * N + y}

    def chip(a, b):
        return {"rows": a * 2 + core, "rep": b}

    up, down = device(z=lax.rem(z + 1, N)), device(z=lax.rem(z + N - 1, N))
    north, south = device(y=lax.rem(y + 1, N)), device(y=lax.rem(y + N - 1, N))
    far_x, near_x, sibling = device(xh=1 - xh), device(xl=1 - xl), device(core=1 - core)
    target_place = lax.rem(rep + SHIFT, Q)
    target = chip(target_place, place)
    source = chip(rep, lax.rem(place + Q - SHIFT, Q))

    barrier = pltpu.get_barrier_semaphore()
    friends = (up, down, north, south, far_x, near_x, sibling, target, source)
    for friend in friends:
        pl.semaphore_signal(barrier, inc=1, device_id=friend, device_id_type=MESH)
    pl.semaphore_wait(barrier, len(friends))

    links = Links(send_sems, recv_sems)
    fbufs, gbufs, parts, terms, xterms = (fbuf0, fbuf1), (gbuf0, gbuf1), (part0, part1), (term0, term1), (xterm0, xterm1)
    first = [
        links.send(feat.at[:, pl.ds(h * TILE, TILE)], fbufs[h].at[core, target_place], target) for h in range(2)
    ]

    @pl.loop(0, NT)
    def _(t):
        sec, i = t // SLOTS, lax.rem(t, SLOTS)
        name = ids[0, sec, i]
        live = i < counts[0, sec]
        kf[t] = jnp.where(live, lax.div(name, Q), -1 - t)
        kb[t] = jnp.where(live, lax.rem(name, Q) + sec * Q, -1 - t)

    def chains(keys, before, last, n_keys):
        @pl.loop(0, NT)
        def _(t):
            best, mine = NT, keys[t]
            for u in range(NT):
                best = jnp.where((keys[u] == mine) & (u < t), u, best)
            before[t] = best

        @pl.loop(0, n_keys)
        def _(i):
            best = NT
            for u in range(NT):
                best = jnp.where(keys[u] == i, u, best)
            last[i] = best

    chains(kf, pf, lf, Q)
    chains(kb, pb, lb, 2 * Q)
    prod[NT] = jnp.zeros((TILE, TILE), F32)

    @pl.loop(0, NT)
    def _(t):
        adj_t[t] = adj[0, t // SLOTS, lax.rem(t, SLOTS)].T

    def share(h):
        copies = []

        def arrived(p):
            chunk = fbufs[h].at[core, pl.ds(p * 2, 2)]
            copies.append(links.send(chunk, chunk, sibling))

        def run():
            first[h].wait_recv()
            yield from gather_ring(links, fbufs[h].at[core], z, xh, up, down, far_x, arrived)
            wait(copies)

        return run()

    def forward(h):
        for sec in range(2):

            @pl.loop(0, SLOTS, unroll=4)
            def _(i):
                slot = lax.rem(lax.rem(ids[0, sec, i], Q) + SHIFT, Q)
                prod[sec * SLOTS + i] = jnp.dot(adj[0, sec, i], fbufs[h][sec, slot], preferred_element_type=F32)

            yield

        @pl.loop(0, NT)
        def _(t):
            prod[t] = prod[t] + prod[pf[t]]

        for off in (4, 3, 5, 2, 6, 1, 7, 0):
            yy = lax.rem(y + off, N)
            for s in range(2):
                parts[h][yy * 2 + s] = prod[lf[s * N + yy]].astype(BF16)
        yield

    def backward(h):
        for sec in range(2):

            @pl.loop(0, SLOTS, unroll=4)
            def _(i):
                tile_row = lax.div(ids[0, sec, i], Q)
                slot = lax.rem(tile_row, N) * 2 + lax.div(tile_row, N)
                t = sec * SLOTS + i
                prod[t] = jnp.dot(adj_t[t], gbufs[h][slot], preferred_element_type=F32)

            yield

        @pl.loop(0, NT)
        def _(t):
            prod[t] = prod[t] + prod[pb[t]]

        yield

    def pair_terms(h):
        copies = {}
        for off in (4, 3, 5, 2, 6, 1, 7, 0):
            zz = lax.rem(z + off, N)
            for s in range(2):
                for sec in range(2):
                    value = prod[lb[sec * Q + zz * 2 + s]].astype(BF16)
                    for half in range(2):
                        terms[h][half, zz * 2 + s, pl.ds(sec * 64, 64)] = value[half * 64 : half * 64 + 64]
            chunk = pl.ds(zz * 2, 2)
            copies[off] = links.send(terms[h].at[1 - core, chunk], xterms[h].at[chunk], sibling)
        return copies

    share0, share1 = share(0), share(1)
    step(share0, 3)
    for _ in range(3):
        step(share0)
        step(share1)
    drain(share0)
    forward0, forward1 = forward(0), forward(1)
    step(forward0)
    step(share1)
    step(forward0)
    step(share1)
    drain(forward0)

    def sum_parts(h, slots, fin):
        return scatter_ring(
            links, parts[h], lambda p: None, *slots, kept.at[h], pairs.at[h, 0], pairs.at[h, 1], y, xl, north, south, near_x, fin
        )

    def set_agg(h):
        def fin(value):
            agg[h] = value.astype(BF16)

        return fin

    sum0 = sum_parts(0, (fl0, fr0), set_agg(0))
    step(sum0)
    drain(share1)
    step(sum0)
    step(forward1)
    step(sum0)
    step(forward1)
    step(sum0)
    drain(forward1)
    sum1 = sum_parts(1, (fl1, fr1), set_agg(1))
    step(sum1)
    drain(sum0, sum1)

    pre = jnp.dot(agg[0], weight[pl.ds(0, TILE)], preferred_element_type=F32)
    pre = pre + jnp.dot(agg[1], weight[pl.ds(TILE, TILE)], preferred_element_type=F32)
    gate = jax.nn.sigmoid(pre)
    act_out[...] = (pre * gate).astype(BF16)
    gpre[...] = (gout[...].astype(F32) * gate * (1.0 + pre * (1.0 - gate))).astype(BF16)
    own = y * 2 + xl
    for h in range(2):
        gbufs[h][own] = lax.dot_general(
            gpre[...], weight[pl.ds(h * TILE, TILE)], (((1,), (1,)), ((), ())), preferred_element_type=F32
        ).astype(BF16)
    grad0 = gather_ring(links, gbuf0, y, xl, north, south, near_x)
    grad1 = gather_ring(links, gbuf1, y, xl, north, south, near_x)
    step(grad0, 2)

    gpre_t = gpre[...].T
    rows = 2 * TILE // Q
    for h in range(2):
        value = jnp.dot(gpre_t, agg[h], preferred_element_type=F32).astype(BF16)
        for p in range(Q):
            wt[(p % N) * 2 + p // N, :, pl.ds(h * TILE, TILE)] = value[p * rows : (p + 1) * rows]

    def weight_gradient():
        def fin(value):
            wsum[0] = value

        yield from scatter_ring(
            links, wt, lambda p: None, wl, wr, wkept, wpair.at[0], wpair.at[1], y, xl, north, south, near_x, fin
        )
        pair = links.send(wsum.at[0], wsum.at[1], sibling)
        yield
        pair.wait_recv()
        wgather[place] = wsum[0] + wsum[1]
        yield from gather_ring(links, wgather, z, xh, up, down, far_x)
        value = wgather[0]
        for q in range(1, Q):
            value = value + wgather[q]
        value = jnp.concatenate([value, jnp.zeros((TILE - rows, 2 * TILE), F32)], axis=0)
        gw_out[...] = value.T[:, :rows]
        yield

    wgrad = weight_gradient()
    step(grad0)
    step(grad1, 2)
    for _ in range(3):
        step(grad0)
        step(grad1)
        step(wgrad)
    drain(grad0)
    backward0, backward1 = backward(0), backward(1)
    step(backward0)
    step(grad1)
    step(wgrad)
    step(backward0)
    drain(grad1)
    step(wgrad)
    drain(backward0)

    def sum_terms(h, slots):
        copies = pair_terms(h)

        def prep(p):
            off = [4, 3, 5, 2, 6, 1, 7, 0][len(used)]
            used.append(off)
            copies[off].wait_recv()
            for s in range(2):
                value = terms[h][core, p * 2 + s].astype(F32) + xterms[h][p * 2 + s].astype(F32)
                terms[h][core, p * 2 + s] = value.astype(BF16)

        used = []

        def fin(value):
            for sec in range(2):
                gf_out[sec, :, pl.ds(h * TILE, TILE)] = value[sec * 64 : sec * 64 + 64]

        return scatter_ring(
            links, terms[h].at[core], prep, *slots, kept_b.at[h], pairs_b.at[h, 0], pairs_b.at[h, 1], z, xh, up, down, far_x, fin
        )

    out0 = sum_terms(0, (bl0, br0))
    step(out0)
    step(backward1)
    step(wgrad)
    step(out0)
    step(backward1)
    step(out0)
    step(wgrad)
    drain(backward1)
    out1 = sum_terms(1, (bl1, br1))
    step(out1)
    drain(out0, out1, wgrad)
    links.finish()


def shards(features, adjacency, tile_ids, tile_counts, weight, grad_out):
    block = (TILE, TILE)
    vmem = pl.BlockSpec(memory_space=pltpu.VMEM)
    smem = pl.BlockSpec(memory_space=pltpu.SMEM)
    rows = 2 * TILE // Q
    slots = pltpu.VMEM((HALF, 2) + block, BF16)
    return pl.pallas_call(
        kernel,
        out_shape=(
            jax.ShapeDtypeStruct((TILE, 2 * TILE), BF16),
            jax.ShapeDtypeStruct((2 * TILE, rows), F32),
            jax.ShapeDtypeStruct((2, 64, 2 * TILE), F32),
        ),
        in_specs=[vmem, vmem, smem, smem, vmem, vmem],
        out_specs=(vmem, vmem, vmem),
        scratch_shapes=[
            pltpu.VMEM((2, Q) + block, BF16),
            pltpu.VMEM((2, Q) + block, BF16),
            pltpu.VMEM((Q,) + block, BF16),
            pltpu.VMEM((Q,) + block, BF16),
            pltpu.VMEM((Q,) + block, BF16),
            pltpu.VMEM((Q,) + block, BF16),
            pltpu.VMEM((2, Q) + block, BF16),
            pltpu.VMEM((2, Q) + block, BF16),
            pltpu.VMEM((Q,) + block, BF16),
            pltpu.VMEM((Q,) + block, BF16),
            pltpu.VMEM((NT,) + block, BF16),
            pltpu.VMEM((NT + 1,) + block, F32),
            pltpu.VMEM((2,) + block, BF16),
            pltpu.VMEM((TILE, 2 * TILE), BF16),
            *([slots] * 8),
            pltpu.VMEM((2,) + block, F32),
            pltpu.VMEM((2, 2) + block, BF16),
            pltpu.VMEM((2,) + block, F32),
            pltpu.VMEM((2, 2) + block, BF16),
            pltpu.VMEM((Q, rows, 2 * TILE), BF16),
            pltpu.VMEM((HALF, 2, rows, 2 * TILE), BF16),
            pltpu.VMEM((HALF, 2, rows, 2 * TILE), BF16),
            pltpu.VMEM((rows, 2 * TILE), F32),
            pltpu.VMEM((2, rows, 2 * TILE), BF16),
            pltpu.VMEM((2, rows, 2 * TILE), F32),
            pltpu.VMEM((Q, rows, 2 * TILE), F32),
            pltpu.SMEM((NT,), jnp.int32),
            pltpu.SMEM((NT,), jnp.int32),
            pltpu.SMEM((NT,), jnp.int32),
            pltpu.SMEM((NT,), jnp.int32),
            pltpu.SMEM((Q,), jnp.int32),
            pltpu.SMEM((2 * Q,), jnp.int32),
            pltpu.SemaphoreType.DMA((N_SEMS,)),
            pltpu.SemaphoreType.DMA((N_SEMS,)),
        ],
        compiler_params=pltpu.CompilerParams(
            collective_id=0, has_side_effects=True, vmem_limit_bytes=40 * 1024 * 1024
        ),
    )(features, adjacency, tile_ids, tile_counts, weight, grad_out)


def solution(mesh):
    return jax.shard_map(
        shards,
        mesh=mesh,
        in_specs=(
            P(("rows", "rep"), None),
            P("rows", "rep", None, None, None),
            P("rows", "rep", None),
            P("rows", "rep"),
            P(),
            P(("rows", "rep"), None),
        ),
        out_specs=(P(("rows", "rep"), None), P(None, "rep"), P("rep", "rows", None)),
        check_vma=False,
    )
```

```python
import jax
import jax.numpy as jnp
from jax import lax
from jax.experimental import pallas as pl
from jax.experimental.pallas import tpu as pltpu
from jax.sharding import PartitionSpec as P

N = 8
Q = 2 * N
HALF = N // 2
TILE = 128
SLOTS = 16
NT = 2 * SLOTS
OFFSETS = (4, 3, 5, 2, 6, 1, 7, 0)
F32 = jnp.float32
BF16 = jnp.bfloat16
MESH = pl.DeviceIdType.MESH
N_SEMS = 185


class Links:
    def __init__(self, send_sems, recv_sems):
        self.send_sems, self.recv_sems, self.copies = send_sems, recv_sems, []

    def send(self, src, dst, device):
        i = len(self.copies)
        assert i < N_SEMS
        copy = pltpu.make_async_remote_copy(
            src_ref=src,
            dst_ref=dst,
            send_sem=self.send_sems.at[i],
            recv_sem=self.recv_sems.at[i],
            device_id=device,
            device_id_type=MESH,
        )
        copy.start()
        self.copies.append(copy)
        return copy

    def finish(self):
        for copy in self.copies:
            copy.wait_send()


def wait(copies):
    for copy in copies:
        copy.wait_recv()


def gather_ring(links, buf, pos, sub, ways, partner, arrived=None):
    own = buf.at[pos * 2 + sub]
    pending = []
    for near, across in ways:
        pending.append([links.send(own, own, near), links.send(own, own, across)])
    pair = links.send(own, own, partner)
    yield
    for k in range(1, HALF):
        for side in range(2):
            p = lax.rem(pos + (N - k, k)[side], N)
            moved = []
            for s in range(2):
                pending[side][s].wait_recv()
                if k < HALF - 1 or s == side:
                    block = buf.at[p * 2 + (sub if s == 0 else 1 - sub)]
                    moved.append(links.send(block, block, ways[side][0]))
            pending[side] = moved
            if arrived:
                arrived(p)
        if k == 1:
            pair.wait_recv()
            if arrived:
                arrived(pos)
        yield
    wait(pending[0] + pending[1])
    if arrived:
        arrived(lax.rem(pos + HALF, N))
    yield


def scatter_ring(links, own, prep, slots, last, pos, sub, ways, partner, done):
    def add(slot, block):
        return (slot.astype(F32) + block.astype(F32)).astype(BF16)

    far = lax.rem(pos + HALF, N)
    prep(far)
    pending = [[links.send(own.at[far * 2 + side], slots.at[side, 0, side], ways[side][0])] for side in range(2)]
    yield
    ending = []
    for k in range(1, HALF):
        for side in range(2):
            p = lax.rem(pos + (HALF - k, N - HALF + k)[side], N)
            prep(p)
            moved = []
            for s in range(2):
                here = slots.at[side, k - 1, s]
                if k == 1 and s != side:
                    here = own.at[p * 2 + s]
                else:
                    pending[side][0 if k == 1 else s].wait_recv()
                    here[...] = add(here[...], own[p * 2 + s])
                if k < HALF - 1:
                    moved.append(links.send(here, slots.at[side, k, s], ways[side][0]))
            if k == HALF - 1:
                for t in range(2):
                    block = slots.at[side, k - 1, sub if t == 0 else 1 - sub]
                    ending.append(links.send(block, last.at[side * 2 + t], ways[side][t]))
            pending[side] = moved
        if k == HALF - 1:
            prep(pos)
            ending.append(links.send(own.at[pos * 2 + 1 - sub], last.at[4], partner))
        yield
    wait(ending)
    value = own[pos * 2 + sub].astype(F32)
    for i in range(5):
        value = value + last[i].astype(F32)
    done(value)
    yield


def drain(*parts):
    parts = list(parts)
    while parts:
        for part in list(parts):
            if next(part, "end") == "end":
                parts.remove(part)


def step(part, count=1):
    for _ in range(count):
        next(part, None)


def kernel(
    feat_in, adj_in, ids_in, counts_in, weight_in, gout_in,
    act_out, gw_out, gf_out,
    feat, adj, weight, gout, fbuf0, fbuf1, gbuf0, gbuf1, part0, part1, term0, term1, xterm0, xterm1, adj_t, prod, agg, gpre,
    fslots0, fslots1, flast0, flast1, bslots0, bslots1, blast0, blast1,
    wt, wslots, wlast, wsum, wgather,
    ids, counts, kf, kb, pf, pb, lf, lb, local_sems, send_sems, recv_sems,
):
    row, rep = lax.axis_index("rows"), lax.axis_index("rep")
    z, xh, core = row // 4, lax.rem(row // 2, 2), lax.rem(row, 2)
    xl, y = rep // N, lax.rem(rep, N)
    place = z * 2 + xh

    loads = [
        pltpu.make_async_copy(src, dst, local_sems.at[i])
        for i, (src, dst) in enumerate(
            [(feat_in.at[:, pl.ds(h * TILE, TILE)], feat.at[h]) for h in range(2)]
            + [(ids_in, ids), (counts_in, counts), (adj_in, adj), (weight_in, weight), (gout_in, gout)]
        )
    ]
    for load in loads:
        load.start()

    def device(z=z, xh=xh, core=core, xl=xl, y=y):
        return {"rows": (z * 2 + xh) * 2 + core, "rep": xl * N + y}

    def turn(value, by):
        return lax.rem(value + by + 2 * N, N)

    up, down = turn(z, 1), turn(z, -1)
    north, south = turn(y, 1), turn(y, -1)
    z_ways = [(device(z=t), device(z=t, xh=1 - xh)) for t in (up, down)]
    y_ways = [(device(y=t), device(y=t, xl=1 - xl)) for t in (north, south)]
    far_x, near_x, sibling = device(xh=1 - xh), device(xl=1 - xl), device(core=1 - core)

    def entry(z, xh, xl, y):
        home = z * 2 + xh
        return turn(z, y - lax.rem(home, N) + HALF), lax.rem(xl + home // N + xh, 2)

    tz, txh = entry(z, xh, xl, y)
    target = device(z=tz, xh=txh, xl=place // N, y=lax.rem(place, N))
    sz, sxh = rep // 2, lax.rem(rep, 2)
    source = device(z=sz, xh=sxh, xl=lax.rem(xh + xl + sxh, 2), y=turn(z, y - sz - HALF))

    barrier = pltpu.get_barrier_semaphore()
    friends = (*z_ways[0], *z_ways[1], *y_ways[0], *y_ways[1], far_x, near_x, sibling, target, source)
    for friend in friends:
        pl.semaphore_signal(barrier, inc=1, device_id=friend, device_id_type=MESH)
    pl.semaphore_wait(barrier, len(friends))

    links = Links(send_sems, recv_sems)
    fbufs, gbufs, parts, terms, xterms = (fbuf0, fbuf1), (gbuf0, gbuf1), (part0, part1), (term0, term1), (xterm0, xterm1)
    first = []
    for h in range(2):
        loads[h].wait()
        first.append(links.send(feat.at[h], fbufs[h].at[core, tz * 2 + txh], target))
    for load in loads[2:]:
        load.wait()

    @pl.loop(0, NT)
    def _(t):
        sec, i = t // SLOTS, lax.rem(t, SLOTS)
        name = ids[0, sec, i]
        live = i < counts[0, sec]
        kf[t] = jnp.where(live, lax.div(name, Q), -1 - t)
        kb[t] = jnp.where(live, lax.rem(name, Q) + sec * Q, -1 - t)

    def chains(keys, before, last, n_keys):
        @pl.loop(0, NT)
        def _(t):
            best, mine = NT, keys[t]
            for u in range(NT):
                best = jnp.where((keys[u] == mine) & (u < t), u, best)
            before[t] = best

        @pl.loop(0, n_keys)
        def _(i):
            best = NT
            for u in range(NT):
                best = jnp.where(keys[u] == i, u, best)
            last[i] = best

    def transpose(sec):
        @pl.loop(0, SLOTS)
        def _(i):
            adj_t[sec * SLOTS + i] = adj[0, sec, i].T

    def share(h):
        copies = []

        def arrived(p):
            chunk = fbufs[h].at[core, pl.ds(p * 2, 2)]
            copies.append(links.send(chunk, chunk, sibling))

        def run():
            first[h].wait_recv()
            yield from gather_ring(links, fbufs[h].at[core], z, xh, z_ways, far_x, arrived)
            wait(copies)

        return run()

    def forward(h):
        for sec in range(2):

            @pl.loop(0, SLOTS, unroll=4)
            def _(i):
                column = lax.rem(ids[0, sec, i], Q)
                ez, exh = entry(sz, sxh, column // N, lax.rem(column, N))
                prod[sec * SLOTS + i] = jnp.dot(adj[0, sec, i], fbufs[h][sec, ez * 2 + exh], preferred_element_type=F32)

            yield

        @pl.loop(0, NT)
        def _(t):
            prod[t] = prod[t] + prod[pf[t]]

        for off in OFFSETS:
            yy = turn(y, off)
            for s in range(2):
                parts[h][yy * 2 + s] = prod[lf[s * N + yy]].astype(BF16)
        yield

    def backward(h):
        for sec in range(2):

            @pl.loop(0, SLOTS, unroll=4)
            def _(i):
                tile_row = lax.div(ids[0, sec, i], Q)
                slot = lax.rem(tile_row, N) * 2 + lax.div(tile_row, N)
                t = sec * SLOTS + i
                prod[t] = jnp.dot(adj_t[t], gbufs[h][slot], preferred_element_type=F32)

            yield

        @pl.loop(0, NT)
        def _(t):
            prod[t] = prod[t] + prod[pb[t]]

        yield

    def pair_terms(h):
        copies = {}
        for off in OFFSETS:
            zz = turn(z, off)
            for s in range(2):
                for sec in range(2):
                    value = prod[lb[sec * Q + zz * 2 + s]].astype(BF16)
                    for half in range(2):
                        terms[h][half, zz * 2 + s, pl.ds(sec * 64, 64)] = value[half * 64 : half * 64 + 64]
            chunk = pl.ds(zz * 2, 2)
            copies[off] = links.send(terms[h].at[1 - core, chunk], xterms[h].at[chunk], sibling)
        return copies

    chains(kf, pf, lf, Q)
    prod[NT] = jnp.zeros((TILE, TILE), F32)
    share0, share1 = share(0), share(1)
    step(share0)
    step(share1)
    chains(kb, pb, lb, 2 * Q)
    step(share0)
    step(share1)
    transpose(0)
    step(share0)
    step(share1)
    transpose(1)
    step(share0)
    step(share1)
    step(share0)
    step(share1)
    drain(share0)

    def sum_parts(h, slots, last):
        def fin(value):
            agg[h] = value.astype(BF16)

        return scatter_ring(links, parts[h], lambda p: None, slots, last, y, xl, y_ways, near_x, fin)

    drain(forward(0))
    sum0 = sum_parts(0, fslots0, flast0)
    step(sum0)
    drain(share1)
    drain(forward(1))
    sum1 = sum_parts(1, fslots1, flast1)
    step(sum1)
    drain(sum0, sum1)

    pre = jnp.dot(agg[0], weight[pl.ds(0, TILE)], preferred_element_type=F32)
    pre = pre + jnp.dot(agg[1], weight[pl.ds(TILE, TILE)], preferred_element_type=F32)
    gate = jax.nn.sigmoid(pre)
    act_out[...] = (pre * gate).astype(BF16)
    gpre[...] = (gout[...].astype(F32) * gate * (1.0 + pre * (1.0 - gate))).astype(BF16)
    own = y * 2 + xl
    grads = []
    for h in range(2):
        gbufs[h][own] = lax.dot_general(
            gpre[...], weight[pl.ds(h * TILE, TILE)], (((1,), (1,)), ((), ())), preferred_element_type=F32
        ).astype(BF16)
        grads.append(gather_ring(links, gbufs[h], y, xl, y_ways, near_x))
        step(grads[h])

    gpre_t = gpre[...].T
    rows = 2 * TILE // Q
    for h in range(2):
        value = jnp.dot(gpre_t, agg[h], preferred_element_type=F32).astype(BF16)
        for p in range(Q):
            wt[(p % N) * 2 + p // N, :, pl.ds(h * TILE, TILE)] = value[p * rows : (p + 1) * rows]

    def weight_gradient():
        def fin(value):
            wsum[0] = value

        yield from scatter_ring(links, wt, lambda p: None, wslots, wlast, y, xl, y_ways, near_x, fin)
        pair = links.send(wsum.at[0], wsum.at[1], sibling)
        yield
        pair.wait_recv()
        wgather[place] = wsum[0] + wsum[1]
        yield from gather_ring(links, wgather, z, xh, z_ways, far_x)
        value = wgather[0]
        for q in range(1, Q):
            value = value + wgather[q]
        gw_out[...] = value
        yield

    wgrad = weight_gradient()
    step(wgrad)
    for _ in range(3):
        step(grads[0])
        step(grads[1])
        step(wgrad)
    drain(grads[0])
    backward0, backward1 = backward(0), backward(1)
    step(backward0)
    drain(grads[1])
    step(wgrad)
    drain(backward0)

    def sum_terms(h, copies, slots, last):
        order = iter(OFFSETS)

        def prep(p):
            copies[next(order)].wait_recv()
            for s in range(2):
                value = terms[h][core, p * 2 + s].astype(F32) + xterms[h][p * 2 + s].astype(F32)
                terms[h][core, p * 2 + s] = value.astype(BF16)

        def fin(value):
            for sec in range(2):
                gf_out[sec, :, pl.ds(h * TILE, TILE)] = value[sec * 64 : sec * 64 + 64]

        return scatter_ring(links, terms[h].at[core], prep, slots, last, z, xh, z_ways, far_x, fin)

    out0 = sum_terms(0, pair_terms(0), bslots0, blast0)
    step(backward1)
    step(out0)
    step(wgrad)
    drain(backward1)
    out1 = sum_terms(1, pair_terms(1), bslots1, blast1)
    step(out0)
    step(out1)
    step(wgrad)
    drain(out0, out1, wgrad)
    links.finish()


def shards(features, adjacency, tile_ids, tile_counts, weight, grad_out):
    block = (TILE, TILE)
    hbm = pl.BlockSpec(memory_space=pltpu.HBM)
    vmem = pl.BlockSpec(memory_space=pltpu.VMEM)
    rows = 2 * TILE // Q
    stripe = (rows, 2 * TILE)
    slots, last = (2, HALF - 1, 2), (5,)
    activated, grad_weight, grad_features = pl.pallas_call(
        kernel,
        out_shape=(
            jax.ShapeDtypeStruct((TILE, 2 * TILE), BF16),
            jax.ShapeDtypeStruct(stripe, F32),
            jax.ShapeDtypeStruct((2, 64, 2 * TILE), F32),
        ),
        in_specs=[hbm] * 6,
        out_specs=(vmem, vmem, vmem),
        scratch_shapes=[
            pltpu.VMEM((2,) + block, BF16),
            pltpu.VMEM((1, 2, SLOTS) + block, BF16),
            pltpu.VMEM((2 * TILE, 2 * TILE), BF16),
            pltpu.VMEM((TILE, 2 * TILE), BF16),
            *[pltpu.VMEM((2, Q) + block, BF16)] * 2,
            *[pltpu.VMEM((Q,) + block, BF16)] * 2,
            *[pltpu.VMEM((Q,) + block, BF16)] * 2,
            *[pltpu.VMEM((2, Q) + block, BF16)] * 2,
            *[pltpu.VMEM((Q,) + block, BF16)] * 2,
            pltpu.VMEM((NT,) + block, BF16),
            pltpu.VMEM((NT + 1,) + block, F32),
            pltpu.VMEM((2,) + block, BF16),
            pltpu.VMEM((TILE, 2 * TILE), BF16),
            *[pltpu.VMEM(slots + block, BF16)] * 2,
            *[pltpu.VMEM(last + block, BF16)] * 2,
            *[pltpu.VMEM(slots + block, BF16)] * 2,
            *[pltpu.VMEM(last + block, BF16)] * 2,
            pltpu.VMEM((Q,) + stripe, BF16),
            pltpu.VMEM(slots + stripe, BF16),
            pltpu.VMEM(last + stripe, BF16),
            pltpu.VMEM((2,) + stripe, F32),
            pltpu.VMEM((Q,) + stripe, F32),
            pltpu.SMEM((1, 2, SLOTS), jnp.int32),
            pltpu.SMEM((1, 2), jnp.int32),
            pltpu.SMEM((NT,), jnp.int32),
            pltpu.SMEM((NT,), jnp.int32),
            pltpu.SMEM((NT,), jnp.int32),
            pltpu.SMEM((NT,), jnp.int32),
            pltpu.SMEM((Q,), jnp.int32),
            pltpu.SMEM((2 * Q,), jnp.int32),
            pltpu.SemaphoreType.DMA((7,)),
            pltpu.SemaphoreType.DMA((N_SEMS,)),
            pltpu.SemaphoreType.DMA((N_SEMS,)),
        ],
        compiler_params=pltpu.CompilerParams(
            collective_id=0, has_side_effects=True, vmem_limit_bytes=63 * 1024 * 1024
        ),
    )(features, adjacency, tile_ids, tile_counts, weight, grad_out)
    return activated, grad_weight.T, grad_features


def solution(mesh):
    return jax.shard_map(
        shards,
        mesh=mesh,
        in_specs=(
            P(("rows", "rep"), None),
            P("rows", "rep", None, None, None),
            P("rows", "rep", None),
            P("rows", "rep"),
            P(),
            P(("rows", "rep"), None),
        ),
        out_specs=(P(("rows", "rep"), None), P(None, "rep"), P("rep", "rows", None)),
        check_vma=False,
    )
```

```python
import jax
import jax.numpy as jnp
from jax import lax
from jax.experimental import pallas as pl
from jax.experimental.pallas import tpu as pltpu
from jax.sharding import PartitionSpec as P

N = 8
Q = 2 * N
HALF = N // 2
TILE = 128
SLOTS = 16
NT = 2 * SLOTS
OFFSETS = (4, 3, 5, 1, 7, 0, 2, 6)
F32 = jnp.float32
BF16 = jnp.bfloat16
MESH = pl.DeviceIdType.MESH
N_SEND = 16
N_RECV = 80


class Links:
    def __init__(self, send_sems, recv_sems):
        self.send_sems, self.recv_sems, self.n_send, self.n_recv = send_sems, recv_sems, 0, 0
        self.finishing = []

    def batch(self, everything):
        sem = self.send_sems.at[self.n_send]
        self.n_send += 1
        assert self.n_send <= N_SEND
        self.finishing.append((everything, sem))
        return sem

    def arrival(self):
        sem = self.recv_sems.at[self.n_recv]
        self.n_recv += 1
        assert self.n_recv <= N_RECV
        return sem

    def send(self, src, dst, device, batch, arrival=None):
        copy = pltpu.make_async_remote_copy(
            src_ref=src,
            dst_ref=dst,
            send_sem=batch,
            recv_sem=self.arrival() if arrival is None else arrival,
            device_id=device,
            device_id_type=MESH,
        )
        copy.start()
        return copy

    def finish(self):
        for everything, sem in self.finishing:
            await_bytes(everything, sem)


def await_bytes(ref, sem):
    pltpu.make_async_copy(ref, ref, sem).wait()


def gather_ring(links, buf, pos, sub, ways, partner, arrived=None):
    own = buf.at[pos * 2 + sub]
    batch = links.batch(buf.at[pl.ds(0, Q - 1)])
    far = [[links.send(own, own, device, batch) for device in ways[1][side]] for side in range(2)]
    close = [links.arrival() for _ in range(2)]
    for side in range(2):
        for device in ways[0][side]:
            links.send(own, own, device, batch, close[side])
    pair = links.send(own, own, partner, batch)
    yield
    three, four = [links.arrival() for _ in range(2)], links.arrival()
    for side in range(2):
        p = lax.rem(pos + (N - 2, 2)[side], N)
        for s in range(2):
            far[side][s].wait_recv()
            block = buf.at[p * 2 + (sub if s == 0 else 1 - sub)]
            if s == side:
                links.send(block, block, ways[1][side][0], batch, four)
            links.send(block, block, ways[0][side][0], batch, three[side])
    if arrived:
        for side in range(2):
            arrived(lax.rem(pos + (N - 2, 2)[side], N))
    yield
    two = buf.at[pl.ds(0, 2)]
    pair.wait_recv()
    if arrived:
        arrived(pos)
    for side in range(2):
        await_bytes(two, close[side])
        if arrived:
            arrived(lax.rem(pos + (N - 1, 1)[side], N))
    yield
    for side in range(2):
        await_bytes(two, three[side])
        if arrived:
            arrived(lax.rem(pos + (N - 3, 3)[side], N))
    await_bytes(two, four)
    if arrived:
        arrived(lax.rem(pos + HALF, N))
    yield


def scatter_ring(links, own, prep, middle, last, pos, sub, ways, partner, done):
    batch, end = links.batch(own.at[pl.ds(0, Q - 1)]), links.arrival()
    halfway = [links.arrival() for _ in range(2)]

    def at(side, distance):
        return lax.rem(pos + (distance, N - distance)[side], N)

    p = at(0, HALF)
    prep(p)
    for side in range(2):
        links.send(own.at[p * 2 + side], middle.at[side, 2], ways[1][side][0], batch, halfway[side])
    for side in range(2):
        p = at(side, 3)
        prep(p)
        links.send(own.at[pl.ds(p * 2, 2)], middle.at[side, pl.ds(0, 2)], ways[0][side][0], batch, halfway[side])
    yield
    for side in range(2):
        p = at(side, 1)
        prep(p)
        for t in range(2):
            block = own.at[p * 2 + (sub if t == 0 else 1 - sub)]
            links.send(block, last.at[side * 4 + t], ways[0][side][t], batch, end)
    prep(pos)
    links.send(own.at[pos * 2 + 1 - sub], last.at[8], partner, batch, end)
    yield
    for side in range(2):
        p = at(side, 2)
        prep(p)
        await_bytes(middle.at[side], halfway[side])
        for s in range(2):
            value = middle[side, s].astype(F32) + own[p * 2 + s].astype(F32)
            if s == side:
                value = value + middle[side, 2].astype(F32)
            middle[side, s] = value.astype(BF16)
        for t in range(2):
            block = middle.at[side, sub if t == 0 else 1 - sub]
            links.send(block, last.at[side * 4 + 2 + t], ways[1][side][t], batch, end)
    yield
    await_bytes(last, end)
    value = own[pos * 2 + sub].astype(F32)
    for i in range(9):
        value = value + last[i].astype(F32)
    done(value)
    yield


def drain(*parts):
    parts = list(parts)
    while parts:
        for part in list(parts):
            if next(part, "end") == "end":
                parts.remove(part)


def step(part, count=1):
    for _ in range(count):
        next(part, None)


def kernel(
    feat_in, adj_in, ids_in, counts_in, weight_in, gout_in,
    act_out, gw_out, gf_out,
    feat, adj, weight, gout, fown0, fown1, fpair0, fpair1, gbuf0, gbuf1, part0, part1, term0, term1, xterm0, xterm1, adj_t, prod, agg, gpre,
    fslots0, fslots1, flast0, flast1, bslots0, bslots1, blast0, blast1,
    wt, wslots, wlast, wsum, wgather,
    ids, counts, table, chains, local_sems, send_sems, recv_sems,
):
    row, rep = lax.axis_index("rows"), lax.axis_index("rep")
    z, xh, core = row // 4, lax.rem(row // 2, 2), lax.rem(row, 2)
    xl, y = rep // N, lax.rem(rep, N)
    place = z * 2 + xh

    loads = [
        pltpu.make_async_copy(src, dst, local_sems.at[i])
        for i, (src, dst) in enumerate(
            [(feat_in.at[:, pl.ds(h * TILE, TILE)], feat.at[h]) for h in range(2)]
            + [(ids_in, ids), (counts_in, counts), (adj_in, adj), (weight_in, weight), (gout_in, gout)]
        )
    ]
    for load in loads:
        load.start()

    def device(z=z, xh=xh, core=core, xl=xl, y=y):
        return {"rows": (z * 2 + xh) * 2 + core, "rep": xl * N + y}

    def turn(value, by):
        return lax.rem(value + by + 2 * N, N)

    z_ways, y_ways = [], []
    for by in (1, 2):
        z_ways.append([(device(z=t), device(z=t, xh=1 - xh)) for t in (turn(z, by), turn(z, -by))])
        y_ways.append([(device(y=t), device(y=t, xl=1 - xl)) for t in (turn(y, by), turn(y, -by))])
    far_x, near_x, sibling = device(xh=1 - xh), device(xl=1 - xl), device(core=1 - core)

    def entry(z, xh, xl, y):
        home = z * 2 + xh
        return turn(z, y - lax.rem(home, N) + HALF), lax.rem(xl + home // N + xh, 2)

    tz, txh = entry(z, xh, xl, y)
    target = device(z=tz, xh=txh, xl=place // N, y=lax.rem(place, N))
    sz, sxh = rep // 2, lax.rem(rep, 2)
    source = device(z=sz, xh=sxh, xl=lax.rem(xh + xl + sxh, 2), y=turn(z, y - sz - HALF))

    barrier = pltpu.get_barrier_semaphore()
    friends = [d for ways in (z_ways, y_ways) for sides in ways for side in sides for d in side]
    friends += [far_x, near_x, sibling, target, source]
    for friend in friends:
        pl.semaphore_signal(barrier, inc=1, device_id=friend, device_id_type=MESH)
    pl.semaphore_wait(barrier, len(friends))

    links = Links(send_sems, recv_sems)
    fowns, fpairs, gbufs, parts = (fown0, fown1), (fpair0, fpair1), (gbuf0, gbuf1), (part0, part1)
    terms, xterms = (term0, term1), (xterm0, xterm1)
    batch = links.batch(feat)
    first = []
    for h in range(2):
        loads[h].wait()
        first.append(links.send(feat.at[h], fowns[h].at[tz * 2 + txh], target, batch))
    for load in loads[2:]:
        load.wait()

    along = [lax.broadcasted_iota(jnp.int32, (NT, TILE), d) for d in range(2)]

    def keys(t):
        name = jnp.zeros((NT, TILE), jnp.int32)
        for i in range(NT):
            name = jnp.where(t == i, ids[0, i // SLOTS, i % SLOTS], name)
        second = t >= SLOTS
        live = t < jnp.where(second, counts[0, 1] + SLOTS, counts[0, 0])
        by_row = jnp.where(live, lax.shift_right_logical(name, 4), -1 - t)
        by_column = jnp.where(live, (name & (Q - 1)) + jnp.where(second, Q, 0), -1 - t)
        return by_row, by_column

    def latest(which):
        t = jnp.max(jnp.where(which, along[0], -1), axis=0, keepdims=True)
        return jnp.where(t < 0, NT, t)

    table_row = lax.broadcasted_iota(jnp.int32, (8, TILE), 0)
    found = jnp.zeros((8, TILE), jnp.int32)
    for i, (down_key, across_key) in enumerate(zip(keys(along[0]), keys(along[1]))):
        before = latest((down_key == across_key) & (along[0] < along[1]))
        found = jnp.where(table_row == 2 * i, before, found)
        found = jnp.where(table_row == 2 * i + 1, latest(down_key == along[1]), found)
    table[...] = found
    chained = pltpu.make_async_copy(table, chains, local_sems.at[7])
    chained.start()

    def transpose(sec):
        @pl.loop(0, SLOTS, unroll=4)
        def _(i):
            adj_t[sec * SLOTS + i] = adj[0, sec, i].T

    def share(h):
        end = links.arrival()
        batch = links.batch(fowns[h])

        def arrived(p):
            chunk = pl.ds(p * 2, 2)
            links.send(fowns[h].at[chunk], fpairs[h].at[chunk], sibling, batch, end)

        def run():
            first[h].wait_recv()
            yield from gather_ring(links, fowns[h], z, xh, z_ways, far_x, arrived)
            await_bytes(fpairs[h], end)
            yield

        return run()

    def forward(h):
        for buf, sec in ((fowns[h], core), (fpairs[h], 1 - core)):

            @pl.loop(0, SLOTS, unroll=4)
            def _(i):
                column = lax.rem(ids[0, sec, i], Q)
                ez, exh = entry(sz, sxh, column // N, lax.rem(column, N))
                prod[sec * SLOTS + i] = jnp.dot(adj[0, sec, i], buf[ez * 2 + exh], preferred_element_type=F32)

            yield

        @pl.loop(0, NT, unroll=2)
        def _(t):
            prod[t] = prod[t] + prod[chains[0, t]]

        for off in OFFSETS:
            yy = turn(y, off)
            for s in range(2):
                parts[h][yy * 2 + s] = prod[chains[1, s * N + yy]].astype(BF16)
        yield

    def backward(h):
        for sec in range(2):

            @pl.loop(0, SLOTS, unroll=4)
            def _(i):
                tile_row = lax.div(ids[0, sec, i], Q)
                slot = lax.rem(tile_row, N) * 2 + lax.div(tile_row, N)
                t = sec * SLOTS + i
                prod[t] = jnp.dot(adj_t[t], gbufs[h][slot], preferred_element_type=F32)

            yield

        @pl.loop(0, NT, unroll=2)
        def _(t):
            prod[t] = prod[t] + prod[chains[2, t]]

        yield

    def pair_terms(h):
        batch = links.batch(xterms[h])
        ends = [links.arrival() for _ in range(5)]
        for off in OFFSETS:
            zz = turn(z, off)
            for s in range(2):
                for sec in range(2):
                    value = prod[chains[3, sec * Q + zz * 2 + s]].astype(BF16)
                    for half in range(2):
                        terms[h][half, zz * 2 + s, pl.ds(sec * 64, 64)] = value[half * 64 : half * 64 + 64]
            chunk = pl.ds(zz * 2, 2)
            links.send(terms[h].at[1 - core, chunk], xterms[h].at[chunk], sibling, batch, ends[min(off, N - off)])
        return ends

    prod[NT] = jnp.zeros((TILE, TILE), F32)
    transpose(0)
    share0, share1 = share(0), share(1)
    step(share0)
    step(share1)
    transpose(1)
    chained.wait()
    step(share0, 2)
    step(share1, 2)
    step(share0)

    def sum_parts(h, slots, last):
        def fin(value):
            agg[h] = value.astype(BF16)

        return scatter_ring(links, parts[h], lambda p: None, slots, last, y, xl, y_ways, near_x, fin)

    forward0, forward1 = forward(0), forward(1)
    step(forward0)
    drain(share0)
    drain(forward0)
    sum0 = sum_parts(0, fslots0, flast0)
    step(sum0, 2)
    step(share1)
    step(forward1)
    drain(share1)
    drain(forward1)
    sum1 = sum_parts(1, fslots1, flast1)
    step(sum1)
    step(sum0)
    step(sum1, 2)
    drain(sum0)
    drain(sum1)

    pre = jnp.dot(agg[0], weight[pl.ds(0, TILE)], preferred_element_type=F32)
    pre = pre + jnp.dot(agg[1], weight[pl.ds(TILE, TILE)], preferred_element_type=F32)
    gate = jax.nn.sigmoid(pre)
    act_out[...] = (pre * gate).astype(BF16)
    gpre[...] = (gout[...].astype(F32) * gate * (1.0 + pre * (1.0 - gate))).astype(BF16)
    own = y * 2 + xl
    grads = []
    for h in range(2):
        gbufs[h][own] = lax.dot_general(
            gpre[...], weight[pl.ds(h * TILE, TILE)], (((1,), (1,)), ((), ())), preferred_element_type=F32
        ).astype(BF16)
        grads.append(gather_ring(links, gbufs[h], y, xl, y_ways, near_x))
        step(grads[h])

    gpre_t = gpre[...].T
    rows = 2 * TILE // Q
    for h in range(2):
        value = jnp.dot(gpre_t, agg[h], preferred_element_type=F32).astype(BF16)
        for p in range(Q):
            wt[(p % N) * 2 + p // N, :, pl.ds(h * TILE, TILE)] = value[p * rows : (p + 1) * rows]

    def weight_gradient():
        pair = []

        def fin(value):
            wsum[0] = value
            pair.append(links.send(wsum.at[0], wsum.at[1], sibling, links.batch(wsum.at[0])))

        yield from scatter_ring(links, wt, lambda p: None, wslots, wlast, y, xl, y_ways, near_x, fin)
        pair[0].wait_recv()
        wgather[place] = wsum[0] + wsum[1]
        yield from gather_ring(links, wgather, z, xh, z_ways, far_x)
        value = wgather[0]
        for q in range(1, Q):
            value = value + wgather[q]
        gw_out[...] = value
        yield

    wgrad = weight_gradient()
    step(wgrad, 2)
    step(grads[0], 2)
    step(grads[1], 2)
    step(wgrad)
    step(grads[0])
    backward0, backward1 = backward(0), backward(1)
    drain(backward0)

    def sum_terms(h, ends, slots, last):
        order = iter(OFFSETS)

        def prep(p):
            off = next(order)
            if off <= HALF:
                await_bytes(xterms[h].at[pl.ds(0, 2 if off in (0, HALF) else 4)], ends[off])
            for s in range(2):
                value = terms[h][core, p * 2 + s].astype(F32) + xterms[h][p * 2 + s].astype(F32)
                terms[h][core, p * 2 + s] = value.astype(BF16)

        def fin(value):
            for sec in range(2):
                gf_out[sec, :, pl.ds(h * TILE, TILE)] = value[sec * 64 : sec * 64 + 64]

        return scatter_ring(links, terms[h].at[core], prep, slots, last, z, xh, z_ways, far_x, fin)

    out0 = sum_terms(0, pair_terms(0), bslots0, blast0)
    step(wgrad)
    step(out0, 2)
    step(wgrad)
    drain(grads[1])
    drain(backward1)
    out1 = sum_terms(1, pair_terms(1), bslots1, blast1)
    step(out0)
    step(out1, 2)
    step(wgrad)
    step(out1)
    step(wgrad)
    drain(out0)
    drain(wgrad)
    drain(out1)
    links.finish()


def shards(features, adjacency, tile_ids, tile_counts, weight, grad_out):
    block = (TILE, TILE)
    hbm = pl.BlockSpec(memory_space=pltpu.HBM)
    vmem = pl.BlockSpec(memory_space=pltpu.VMEM)
    rows = 2 * TILE // Q
    stripe = (rows, 2 * TILE)
    slots, last = (2, 3), (9,)
    activated, grad_weight, grad_features = pl.pallas_call(
        kernel,
        out_shape=(
            pltpu.VMEM((TILE, 2 * TILE), BF16),
            pltpu.VMEM(stripe, F32),
            pltpu.VMEM((2, 64, 2 * TILE), F32),
        ),
        in_specs=[hbm] * 6,
        out_specs=(vmem, vmem, vmem),
        scratch_shapes=[
            pltpu.VMEM((2,) + block, BF16),
            pltpu.VMEM((1, 2, SLOTS) + block, BF16),
            pltpu.VMEM((2 * TILE, 2 * TILE), BF16),
            pltpu.VMEM((TILE, 2 * TILE), BF16),
            *[pltpu.VMEM((Q,) + block, BF16)] * 4,
            *[pltpu.VMEM((Q,) + block, BF16)] * 2,
            *[pltpu.VMEM((Q,) + block, BF16)] * 2,
            *[pltpu.VMEM((2, Q) + block, BF16)] * 2,
            *[pltpu.VMEM((Q,) + block, BF16)] * 2,
            pltpu.VMEM((NT,) + block, BF16),
            pltpu.VMEM((NT + 1,) + block, F32),
            pltpu.VMEM((2,) + block, BF16),
            pltpu.VMEM((TILE, 2 * TILE), BF16),
            *[pltpu.VMEM(slots + block, BF16)] * 2,
            *[pltpu.VMEM(last + block, BF16)] * 2,
            *[pltpu.VMEM(slots + block, BF16)] * 2,
            *[pltpu.VMEM(last + block, BF16)] * 2,
            pltpu.VMEM((Q,) + stripe, BF16),
            pltpu.VMEM(slots + stripe, BF16),
            pltpu.VMEM(last + stripe, BF16),
            pltpu.VMEM((2,) + stripe, F32),
            pltpu.VMEM((Q,) + stripe, F32),
            pltpu.SMEM((1, 2, SLOTS), jnp.int32),
            pltpu.SMEM((1, 2), jnp.int32),
            pltpu.VMEM((8, TILE), jnp.int32),
            pltpu.SMEM((8, TILE), jnp.int32),
            pltpu.SemaphoreType.DMA((8,)),
            pltpu.SemaphoreType.DMA((N_SEND,)),
            pltpu.SemaphoreType.DMA((N_RECV,)),
        ],
        compiler_params=pltpu.CompilerParams(
            collective_id=0, has_side_effects=True, vmem_limit_bytes=40 * 1024 * 1024
        ),
    )(*[pltpu.with_memory_space_constraint(x, pltpu.HBM) for x in (features, adjacency, tile_ids, tile_counts, weight, grad_out)])
    return activated, grad_weight.T, grad_features


def solution(mesh):
    return jax.shard_map(
        shards,
        mesh=mesh,
        in_specs=(
            P(("rows", "rep"), None),
            P("rows", "rep", None, None, None),
            P("rows", "rep", None),
            P("rows", "rep"),
            P(),
            P(("rows", "rep"), None),
        ),
        out_specs=(P(("rows", "rep"), None), P(None, "rep"), P("rep", "rows", None)),
        check_vma=False,
    )
```

```python
import jax
import jax.numpy as jnp
from jax import lax
from jax.experimental import pallas as pl
from jax.experimental.pallas import tpu as pltpu
from jax.sharding import PartitionSpec as P

N = 8
Q = 2 * N
HALF = N // 2
TILE = 128
SLOTS = 16
NT = 2 * SLOTS
OFFSETS = (4, 3, 5, 2, 6, 1, 7, 0)
F32 = jnp.float32
BF16 = jnp.bfloat16
MESH = pl.DeviceIdType.MESH
N_SEND = 17
N_RECV = 112


class Links:
    def __init__(self, send_sems, recv_sems):
        self.send_sems, self.recv_sems, self.n_send, self.n_recv = send_sems, recv_sems, 0, 0
        self.finishing = []

    def batch(self, everything):
        sem = self.send_sems.at[self.n_send]
        self.n_send += 1
        assert self.n_send <= N_SEND
        self.finishing.append((everything, sem))
        return sem

    def arrival(self):
        sem = self.recv_sems.at[self.n_recv]
        self.n_recv += 1
        assert self.n_recv <= N_RECV
        return sem

    def send(self, src, dst, device, batch, arrival=None):
        copy = pltpu.make_async_remote_copy(
            src_ref=src,
            dst_ref=dst,
            send_sem=batch,
            recv_sem=self.arrival() if arrival is None else arrival,
            device_id=device,
            device_id_type=MESH,
        )
        copy.start()
        return copy

    def finish(self):
        for everything, sem in self.finishing:
            await_bytes(everything, sem)


def await_bytes(ref, sem):
    pltpu.make_async_copy(ref, ref, sem).wait()


def gather_ring(links, buf, pos, sub, ways, partner, arrived=None):
    own = buf.at[pos * 2 + sub]
    batch = links.batch(buf.at[pl.ds(0, Q - 1)])
    one = [[links.send(own, own, device, batch) for device in ways[0][side]] for side in range(2)]
    pair = links.send(own, own, partner, batch)
    yield

    def blocks(side, distance):
        p = lax.rem(pos + (N - distance, distance)[side], N)
        return p, [buf.at[p * 2 + (sub if s == 0 else 1 - sub)] for s in range(2)]

    two = []
    for side in range(2):
        p, came = blocks(side, 1)
        moved = []
        for s in range(2):
            one[side][s].wait_recv()
            moved.append(links.send(came[s], came[s], ways[0][side][0], batch))
        two.append(moved)
        if arrived:
            arrived(p)
    yield
    three, four = [links.arrival() for _ in range(2)], links.arrival()
    for side in range(2):
        p, came = blocks(side, 2)
        for s in range(2):
            two[side][s].wait_recv()
            if s == side:
                links.send(came[s], came[s], ways[1][side][0], batch, four)
            links.send(came[s], came[s], ways[0][side][0], batch, three[side])
        if arrived:
            arrived(p)
    pair.wait_recv()
    if arrived:
        arrived(pos)
    yield
    for side in range(2):
        await_bytes(buf.at[pl.ds(0, 2)], three[side])
        if arrived:
            arrived(blocks(side, 3)[0])
    await_bytes(buf.at[pl.ds(0, 2)], four)
    if arrived:
        arrived(lax.rem(pos + HALF, N))
    yield


def scatter_ring(links, own, prep, slots, last, pos, sub, ways, partner, done):
    batch, end = links.batch(own.at[pl.ds(0, Q - 1)]), links.arrival()
    at_two, at_one = [links.arrival() for _ in range(2)], [links.arrival() for _ in range(2)]

    def at(side, distance):
        return lax.rem(pos + (distance, N - distance)[side], N)

    p = at(0, HALF)
    prep(p)
    for side in range(2):
        links.send(own.at[p * 2 + side], slots.at[side, 2], ways[1][side][0], batch, at_two[side])
    for side in range(2):
        p = at(side, 3)
        prep(p)
        links.send(own.at[pl.ds(p * 2, 2)], slots.at[side, pl.ds(0, 2)], ways[0][side][0], batch, at_two[side])
    yield
    for side in range(2):
        p = at(side, 2)
        prep(p)
        await_bytes(slots.at[side, pl.ds(0, 3)], at_two[side])
        for s in range(2):
            value = slots[side, s].astype(F32) + own[p * 2 + s].astype(F32)
            if s == side:
                value = value + slots[side, 2].astype(F32)
            slots[side, s] = value.astype(BF16)
        links.send(slots.at[side, pl.ds(0, 2)], slots.at[side, pl.ds(3, 2)], ways[0][side][0], batch, at_one[side])
    yield
    for side in range(2):
        p = at(side, 1)
        prep(p)
        await_bytes(slots.at[side, pl.ds(3, 2)], at_one[side])
        for s in range(2):
            slots[side, 3 + s] = (slots[side, 3 + s].astype(F32) + own[p * 2 + s].astype(F32)).astype(BF16)
        for t in (1, 0):
            block = slots.at[side, 3 + (sub if t == 0 else 1 - sub)]
            links.send(block, last.at[side * 2 + t], ways[0][side][t], batch, end)
    prep(pos)
    links.send(own.at[pos * 2 + 1 - sub], last.at[4], partner, batch, end)
    yield
    await_bytes(last, end)
    value = own[pos * 2 + sub].astype(F32)
    for i in range(5):
        value = value + last[i].astype(F32)
    done(value)
    yield


def drain(*parts):
    parts = list(parts)
    while parts:
        for part in list(parts):
            if next(part, "end") == "end":
                parts.remove(part)


def step(part, count=1):
    for _ in range(count):
        next(part, None)


def kernel(
    feat_in, adj_in, ids_in, counts_in, weight_in, gout_in,
    act_out, gw_out, gf_out,
    feat, adj, weight, gout, fown0, fown1, fpair0, fpair1, gbuf0, gbuf1, part0, part1, term0, term1, xterm0, xterm1, adj_t, prod, agg, gpre,
    fslots0, fslots1, flast0, flast1, bslots0, bslots1, blast0, blast1,
    wt, wpair, wslots, wlast, wsum, wgather,
    ids, counts, table, chains, local_sems, send_sems, recv_sems,
):
    row, rep = lax.axis_index("rows"), lax.axis_index("rep")
    z, xh, core = row // 4, lax.rem(row // 2, 2), lax.rem(row, 2)
    xl, y = rep // N, lax.rem(rep, N)
    place = z * 2 + xh

    loads = [
        pltpu.make_async_copy(src, dst, local_sems.at[i])
        for i, (src, dst) in enumerate(
            [(feat_in.at[:, pl.ds(h * TILE, TILE)], feat.at[h]) for h in range(2)]
            + [(ids_in, ids), (counts_in, counts), (adj_in, adj), (weight_in, weight), (gout_in, gout)]
        )
    ]
    for load in loads:
        load.start()

    def device(z=z, xh=xh, core=core, xl=xl, y=y):
        return {"rows": (z * 2 + xh) * 2 + core, "rep": xl * N + y}

    def turn(value, by):
        return lax.rem(value + by + 2 * N, N)

    z_ways, y_ways = [], []
    for by in (1, 2):
        z_ways.append([(device(z=t), device(z=t, xh=1 - xh)) for t in (turn(z, by), turn(z, -by))])
        y_ways.append([(device(y=t), device(y=t, xl=1 - xl)) for t in (turn(y, by), turn(y, -by))])
    far_x, near_x, sibling = device(xh=1 - xh), device(xl=1 - xl), device(core=1 - core)

    def entry(z, xh, xl, y):
        home = z * 2 + xh
        return turn(z, y - lax.rem(home, N) + HALF), lax.rem(xl + home // N + xh, 2)

    tz, txh = entry(z, xh, xl, y)
    target = device(z=tz, xh=txh, xl=place // N, y=lax.rem(place, N))
    sz, sxh = rep // 2, lax.rem(rep, 2)
    source = device(z=sz, xh=sxh, xl=lax.rem(xh + xl + sxh, 2), y=turn(z, y - sz - HALF))

    barrier = pltpu.get_barrier_semaphore()
    friends = [d for ways in (z_ways, y_ways) for sides in ways for side in sides for d in side]
    friends += [far_x, near_x, sibling, target, source]
    for friend in friends:
        pl.semaphore_signal(barrier, inc=1, device_id=friend, device_id_type=MESH)
    pl.semaphore_wait(barrier, len(friends))

    links = Links(send_sems, recv_sems)
    fowns, fpairs, gbufs, parts = (fown0, fown1), (fpair0, fpair1), (gbuf0, gbuf1), (part0, part1)
    terms, xterms = (term0, term1), (xterm0, xterm1)
    batch = links.batch(feat)
    first = []
    for h in range(2):
        loads[h].wait()
        first.append(links.send(feat.at[h], fowns[h].at[tz * 2 + txh], target, batch))
    for load in loads[2:]:
        load.wait()

    along = [lax.broadcasted_iota(jnp.int32, (NT, TILE), d) for d in range(2)]

    def keys(t):
        name = jnp.zeros((NT, TILE), jnp.int32)
        for i in range(NT):
            name = jnp.where(t == i, ids[0, i // SLOTS, i % SLOTS], name)
        second = t >= SLOTS
        live = t < jnp.where(second, counts[0, 1] + SLOTS, counts[0, 0])
        by_row = jnp.where(live, lax.shift_right_logical(name, 4), -1 - t)
        by_column = jnp.where(live, (name & (Q - 1)) + jnp.where(second, Q, 0), -1 - t)
        return by_row, by_column

    def latest(which):
        t = jnp.max(jnp.where(which, along[0], -1), axis=0, keepdims=True)
        return jnp.where(t < 0, NT, t)

    table_row = lax.broadcasted_iota(jnp.int32, (8, TILE), 0)
    found = jnp.zeros((8, TILE), jnp.int32)
    for i, (down_key, across_key) in enumerate(zip(keys(along[0]), keys(along[1]))):
        before = latest((down_key == across_key) & (along[0] < along[1]))
        found = jnp.where(table_row == 2 * i, before, found)
        found = jnp.where(table_row == 2 * i + 1, latest(down_key == along[1]), found)
    table[...] = found
    chained = pltpu.make_async_copy(table, chains, local_sems.at[7])
    chained.start()

    def transpose(sec):
        @pl.loop(0, SLOTS, unroll=4)
        def _(i):
            adj_t[sec * SLOTS + i] = adj[0, sec, i].T

    def share(h):
        end = links.arrival()
        batch = links.batch(fowns[h])

        def arrived(p):
            chunk = pl.ds(p * 2, 2)
            links.send(fowns[h].at[chunk], fpairs[h].at[chunk], sibling, batch, end)

        def run():
            first[h].wait_recv()
            yield from gather_ring(links, fowns[h], z, xh, z_ways, far_x, arrived)
            await_bytes(fpairs[h], end)
            yield

        return run()

    def forward(h):
        for buf, sec in ((fowns[h], core), (fpairs[h], 1 - core)):

            @pl.loop(0, SLOTS, unroll=4)
            def _(i):
                column = lax.rem(ids[0, sec, i], Q)
                ez, exh = entry(sz, sxh, column // N, lax.rem(column, N))
                prod[sec * SLOTS + i] = jnp.dot(adj[0, sec, i], buf[ez * 2 + exh], preferred_element_type=F32)

            yield

        @pl.loop(0, NT, unroll=2)
        def _(t):
            prod[t] = prod[t] + prod[chains[0, t]]

        for off in OFFSETS:
            yy = turn(y, off)
            for s in range(2):
                parts[h][yy * 2 + s] = prod[chains[1, s * N + yy]].astype(BF16)
        yield

    def backward(h):
        for sec in range(2):

            @pl.loop(0, SLOTS, unroll=4)
            def _(i):
                tile_row = lax.div(ids[0, sec, i], Q)
                slot = lax.rem(tile_row, N) * 2 + lax.div(tile_row, N)
                t = sec * SLOTS + i
                prod[t] = jnp.dot(adj_t[t], gbufs[h][slot], preferred_element_type=F32)

            yield

        @pl.loop(0, NT, unroll=2)
        def _(t):
            prod[t] = prod[t] + prod[chains[2, t]]

        yield

    def pair_terms(h):
        batch = links.batch(xterms[h])
        ends = [links.arrival() for _ in range(5)]
        for off in OFFSETS:
            zz = turn(z, off)
            for s in range(2):
                for sec in range(2):
                    value = prod[chains[3, sec * Q + zz * 2 + s]].astype(BF16)
                    for half in range(2):
                        terms[h][half, zz * 2 + s, pl.ds(sec * 64, 64)] = value[half * 64 : half * 64 + 64]
            chunk = pl.ds(zz * 2, 2)
            links.send(terms[h].at[1 - core, chunk], xterms[h].at[chunk], sibling, batch, ends[min(off, N - off)])
        return ends

    prod[NT] = jnp.zeros((TILE, TILE), F32)
    share0, share1 = share(0), share(1)
    step(share0)
    transpose(0)
    step(share1)
    transpose(1)
    chained.wait()
    for _ in range(2):
        step(share0)
        step(share1)
    step(share0)

    def sum_parts(h, slots, last):
        def fin(value):
            agg[h] = value.astype(BF16)

        return scatter_ring(links, parts[h], lambda p: None, slots, last, y, xl, y_ways, near_x, fin)

    forward0, forward1 = forward(0), forward(1)
    step(forward0)
    drain(share0)
    drain(forward0)
    sum0 = sum_parts(0, fslots0, flast0)
    step(sum0)
    step(share1)
    step(forward1)
    drain(share1)
    drain(forward1)
    sum1 = sum_parts(1, fslots1, flast1)
    for _ in range(2):
        step(sum1)
        step(sum0)
    step(sum1)
    drain(sum0)
    drain(sum1)

    pre = jnp.dot(agg[0], weight[pl.ds(0, TILE)], preferred_element_type=F32)
    pre = pre + jnp.dot(agg[1], weight[pl.ds(TILE, TILE)], preferred_element_type=F32)
    gate = jax.nn.sigmoid(pre)
    act_out[...] = (pre * gate).astype(BF16)
    gpre[...] = (gout[...].astype(F32) * gate * (1.0 + pre * (1.0 - gate))).astype(BF16)
    own = y * 2 + xl
    grads = []
    for h in range(2):
        gbufs[h][own] = lax.dot_general(
            gpre[...], weight[pl.ds(h * TILE, TILE)], (((1,), (1,)), ((), ())), preferred_element_type=F32
        ).astype(BF16)
        grads.append(gather_ring(links, gbufs[h], y, xl, y_ways, near_x))
        step(grads[h])

    gpre_t = gpre[...].T
    rows = 2 * TILE // Q
    for h in range(2):
        value = jnp.dot(gpre_t, agg[h], preferred_element_type=F32).astype(BF16)
        for p in range(Q):
            wt[h, (p % N) * 2 + p // N] = value[p * rows : (p + 1) * rows]

    def weight_gradient():
        pair = links.send(wt.at[1 - core], wpair, sibling, links.batch(wpair))
        yield
        pair.wait_recv()
        for q in range(Q):
            wt[core, q] = (wt[core, q].astype(F32) + wpair[q].astype(F32)).astype(BF16)

        def fin(value):
            wgather[place] = value.astype(BF16)

        ring = scatter_ring(links, wt.at[core], lambda p: None, wslots, wlast, y, xl, y_ways, near_x, fin)
        for _ in range(3):
            step(ring)
            yield
        drain(ring)
        ring = gather_ring(links, wgather, z, xh, z_ways, far_x)
        for _ in range(3):
            step(ring)
            yield
        drain(ring)
        value = wgather[0].astype(F32)
        for q in range(1, Q):
            value = value + wgather[q].astype(F32)
        wsum[core] = value
        half = wsum.at[core]
        pair = links.send(half, half, sibling, links.batch(half))
        yield
        pair.wait_recv()
        for h in range(2):
            gw_out[:, pl.ds(h * TILE, TILE)] = wsum[h]
        yield

    wgrad = weight_gradient()
    step(wgrad)
    step(grads[0])
    step(wgrad)
    step(grads[1])
    step(grads[0])
    step(grads[1])
    step(wgrad)
    step(grads[0])
    backward0, backward1 = backward(0), backward(1)
    drain(backward0)

    def sum_terms(h, ends, slots, last):
        order = iter(OFFSETS)

        def prep(p):
            off = next(order)
            if off <= HALF:
                await_bytes(xterms[h].at[pl.ds(0, 2 if off in (0, HALF) else 4)], ends[off])
            for s in range(2):
                value = terms[h][core, p * 2 + s].astype(F32) + xterms[h][p * 2 + s].astype(F32)
                terms[h][core, p * 2 + s] = value.astype(BF16)

        def fin(value):
            for sec in range(2):
                gf_out[sec, :, pl.ds(h * TILE, TILE)] = value[sec * 64 : sec * 64 + 64]

        return scatter_ring(links, terms[h].at[core], prep, slots, last, z, xh, z_ways, far_x, fin)

    out0 = sum_terms(0, pair_terms(0), bslots0, blast0)
    step(wgrad)
    step(out0)
    drain(grads[1])
    drain(backward1)
    step(wgrad)
    out1 = sum_terms(1, pair_terms(1), bslots1, blast1)
    step(out0)
    step(out1)
    step(wgrad)
    step(out0)
    step(out1)
    step(wgrad)
    drain(out0)
    step(out1)
    step(wgrad)
    drain(out1)
    drain(wgrad)
    links.finish()


def shards(features, adjacency, tile_ids, tile_counts, weight, grad_out):
    block = (TILE, TILE)
    hbm = pl.BlockSpec(memory_space=pltpu.HBM)
    vmem = pl.BlockSpec(memory_space=pltpu.VMEM)
    rows = 2 * TILE // Q
    stripe, part = (rows, 2 * TILE), (rows, TILE)
    slots, last = (2, 5), (5,)
    activated, grad_weight, grad_features = pl.pallas_call(
        kernel,
        out_shape=(
            pltpu.VMEM((TILE, 2 * TILE), BF16),
            pltpu.VMEM(stripe, F32),
            pltpu.VMEM((2, 64, 2 * TILE), F32),
        ),
        in_specs=[hbm] * 6,
        out_specs=(vmem, vmem, vmem),
        scratch_shapes=[
            pltpu.VMEM((2,) + block, BF16),
            pltpu.VMEM((1, 2, SLOTS) + block, BF16),
            pltpu.VMEM((2 * TILE, 2 * TILE), BF16),
            pltpu.VMEM((TILE, 2 * TILE), BF16),
            *[pltpu.VMEM((Q,) + block, BF16)] * 4,
            *[pltpu.VMEM((Q,) + block, BF16)] * 2,
            *[pltpu.VMEM((Q,) + block, BF16)] * 2,
            *[pltpu.VMEM((2, Q) + block, BF16)] * 2,
            *[pltpu.VMEM((Q,) + block, BF16)] * 2,
            pltpu.VMEM((NT,) + block, BF16),
            pltpu.VMEM((NT + 1,) + block, F32),
            pltpu.VMEM((2,) + block, BF16),
            pltpu.VMEM((TILE, 2 * TILE), BF16),
            *[pltpu.VMEM(slots + block, BF16)] * 2,
            *[pltpu.VMEM(last + block, BF16)] * 2,
            *[pltpu.VMEM(slots + block, BF16)] * 2,
            *[pltpu.VMEM(last + block, BF16)] * 2,
            pltpu.VMEM((2, Q) + part, BF16),
            pltpu.VMEM((Q,) + part, BF16),
            pltpu.VMEM(slots + part, BF16),
            pltpu.VMEM(last + part, BF16),
            pltpu.VMEM((2,) + part, F32),
            pltpu.VMEM((Q,) + part, BF16),
            pltpu.SMEM((1, 2, SLOTS), jnp.int32),
            pltpu.SMEM((1, 2), jnp.int32),
            pltpu.VMEM((8, TILE), jnp.int32),
            pltpu.SMEM((8, TILE), jnp.int32),
            pltpu.SemaphoreType.DMA((8,)),
            pltpu.SemaphoreType.DMA((N_SEND,)),
            pltpu.SemaphoreType.DMA((N_RECV,)),
        ],
        compiler_params=pltpu.CompilerParams(
            collective_id=0, has_side_effects=True, vmem_limit_bytes=40 * 1024 * 1024
        ),
    )(*[pltpu.with_memory_space_constraint(x, pltpu.HBM) for x in (features, adjacency, tile_ids, tile_counts, weight, grad_out)])
    return activated, grad_weight.T, grad_features


def solution(mesh):
    return jax.shard_map(
        shards,
        mesh=mesh,
        in_specs=(
            P(("rows", "rep"), None),
            P("rows", "rep", None, None, None),
            P("rows", "rep", None),
            P("rows", "rep"),
            P(),
            P(("rows", "rep"), None),
        ),
        out_specs=(P(("rows", "rep"), None), P(None, "rep"), P("rep", "rows", None)),
        check_vma=False,
    )
```

```python
import jax
import jax.numpy as jnp
from jax import lax
from jax.experimental import pallas as pl
from jax.experimental.pallas import tpu as pltpu
from jax.sharding import PartitionSpec as P

N = 8
Q = 2 * N
HALF = N // 2
TILE = 128
SLOTS = 16
NT = 2 * SLOTS
OFFSETS = (4, 3, 5, 2, 6, 1, 7, 0)
F32 = jnp.float32
BF16 = jnp.bfloat16
MESH = pl.DeviceIdType.MESH
N_SEND = 17
N_RECV = 83


class Links:
    def __init__(self, send_sems, recv_sems):
        self.send_sems, self.recv_sems, self.n_send, self.n_recv = send_sems, recv_sems, 0, 0
        self.finishing = []

    def batch(self, everything):
        sem = self.send_sems.at[self.n_send]
        self.n_send += 1
        assert self.n_send <= N_SEND
        self.finishing.append((everything, sem))
        return sem

    def arrival(self):
        sem = self.recv_sems.at[self.n_recv]
        self.n_recv += 1
        assert self.n_recv <= N_RECV
        return sem

    def send(self, src, dst, device, batch, arrival=None):
        copy = pltpu.make_async_remote_copy(
            src_ref=src,
            dst_ref=dst,
            send_sem=batch,
            recv_sem=self.arrival() if arrival is None else arrival,
            device_id=device,
            device_id_type=MESH,
        )
        copy.start()
        return copy

    def finish(self):
        for everything, sem in self.finishing:
            await_bytes(everything, sem)


def await_bytes(ref, sem):
    pltpu.make_async_copy(ref, ref, sem).wait()


def gather_ring(links, buf, pos, sub, ways, partner, straight=False, arrived=None):
    own, two_blocks = buf.at[pos * 2 + sub], buf.at[pl.ds(0, 2)]
    batch = links.batch(buf.at[pl.ds(0, Q - 1)])
    came = [[links.arrival() for _ in range(2)] for _ in range(3)]
    four, pair = links.arrival(), links.arrival()

    def position(side, distance):
        return lax.rem(pos + (N - distance, distance)[side], N)

    for distance in (2, 1) if straight else (1,):
        for t in (1, 0):
            for side in range(2):
                links.send(own, own, ways[distance - 1][side][t], batch, came[distance - 1][side])
    links.send(own, own, partner, batch, pair)
    yield

    def first():
        for side in range(2):
            p = position(side, 1)
            await_bytes(two_blocks, came[0][side])
            if not straight:
                chunk = buf.at[pl.ds(p * 2, 2)]
                links.send(chunk, chunk, ways[0][side][0], batch, came[1][side])
        if arrived:
            for side in range(2):
                arrived(position(side, 1))

    if not straight:
        first()
        yield
    for side in range(2):
        p = position(side, 2)
        await_bytes(two_blocks, came[1][side])
        block, chunk = buf.at[p * 2 + (sub if side == 0 else 1 - sub)], buf.at[pl.ds(p * 2, 2)]
        links.send(block, block, ways[1][side][0], batch, four)
        links.send(chunk, chunk, ways[0][side][0], batch, came[2][side])
    if arrived:
        for side in range(2):
            arrived(position(side, 2))
    if straight:
        yield
        first()
    await_bytes(own, pair)
    if arrived:
        arrived(pos)
    yield
    for side in range(2):
        await_bytes(two_blocks, came[2][side])
        if arrived:
            arrived(position(side, 3))
    await_bytes(two_blocks, four)
    if arrived:
        arrived(position(0, HALF))
    yield


def scatter_ring(links, own, prep, slots, last, pos, sub, ways, partner, done):
    batch, end = links.batch(own.at[pl.ds(0, Q - 1)]), links.arrival()
    at_two, at_one = [links.arrival() for _ in range(2)], [links.arrival() for _ in range(2)]

    def at(side, distance):
        return lax.rem(pos + (distance, N - distance)[side], N)

    p = at(0, HALF)
    prep(p)
    for side in range(2):
        links.send(own.at[p * 2 + side], slots.at[side, 2], ways[1][side][0], batch, at_two[side])
    for side in range(2):
        p = at(side, 3)
        prep(p)
        links.send(own.at[pl.ds(p * 2, 2)], slots.at[side, pl.ds(0, 2)], ways[0][side][0], batch, at_two[side])
    yield
    for side in range(2):
        p = at(side, 2)
        prep(p)
        await_bytes(slots.at[side, pl.ds(0, 3)], at_two[side])
        for s in range(2):
            value = slots[side, s].astype(F32) + own[p * 2 + s].astype(F32)
            if s == side:
                value = value + slots[side, 2].astype(F32)
            slots[side, s] = value.astype(BF16)
        links.send(slots.at[side, pl.ds(0, 2)], slots.at[side, pl.ds(3, 2)], ways[0][side][0], batch, at_one[side])
    yield
    for side in range(2):
        p = at(side, 1)
        prep(p)
        await_bytes(slots.at[side, pl.ds(3, 2)], at_one[side])
        for s in range(2):
            slots[side, 3 + s] = (slots[side, 3 + s].astype(F32) + own[p * 2 + s].astype(F32)).astype(BF16)
        for t in (1, 0):
            block = slots.at[side, 3 + (sub if t == 0 else 1 - sub)]
            links.send(block, last.at[side * 2 + t], ways[0][side][t], batch, end)
    prep(pos)
    links.send(own.at[pos * 2 + 1 - sub], last.at[4], partner, batch, end)
    yield
    await_bytes(last, end)
    value = own[pos * 2 + sub].astype(F32)
    for i in range(5):
        value = value + last[i].astype(F32)
    done(value)
    yield


def drain(*parts):
    parts = list(parts)
    while parts:
        for part in list(parts):
            if next(part, "end") == "end":
                parts.remove(part)


def step(part, count=1):
    for _ in range(count):
        next(part, None)


def kernel(
    feat_in, adj_in, ids_in, counts_in, weight_in, gout_in,
    act_out, gw_out, gf_out,
    feat, adj, weight, gout, fown0, fown1, fpair0, fpair1, gbuf0, gbuf1, part0, part1, term0, term1, xterm0, xterm1, adj_t, prod0, prod1, agg, gpre,
    fslots0, fslots1, flast0, flast1, bslots0, bslots1, blast0, blast1,
    wt, wpair, wslots, wlast, wsum, wgather,
    ids, counts, table, chains, local_sems, send_sems, recv_sems,
):
    row, rep = lax.axis_index("rows"), lax.axis_index("rep")
    z, xh, core = row // 4, lax.rem(row // 2, 2), lax.rem(row, 2)
    xl, y = rep // N, lax.rem(rep, N)
    place = z * 2 + xh

    loads = [
        pltpu.make_async_copy(src, dst, local_sems.at[i])
        for i, (src, dst) in enumerate(
            [(feat_in.at[:, pl.ds(h * TILE, TILE)], feat.at[h]) for h in range(2)]
            + [(ids_in, ids), (counts_in, counts), (adj_in, adj), (weight_in, weight), (gout_in, gout)]
        )
    ]
    for load in loads[:2]:
        load.start()

    def device(z=z, xh=xh, core=core, xl=xl, y=y):
        return {"rows": (z * 2 + xh) * 2 + core, "rep": xl * N + y}

    def turn(value, by):
        return lax.rem(value + by + 2 * N, N)

    z_ways, y_ways = [], []
    for by in (1, 2):
        z_ways.append([(device(z=t), device(z=t, xh=1 - xh)) for t in (turn(z, by), turn(z, -by))])
        y_ways.append([(device(y=t), device(y=t, xl=1 - xl)) for t in (turn(y, by), turn(y, -by))])
    far_x, near_x, sibling = device(xh=1 - xh), device(xl=1 - xl), device(core=1 - core)

    def entry(z, xh, xl, y):
        home = z * 2 + xh
        return turn(z, y - lax.rem(home, N) + HALF), lax.rem(xl + home // N + xh, 2)

    tz, txh = entry(z, xh, xl, y)
    target = device(z=tz, xh=txh, xl=place // N, y=lax.rem(place, N))
    sz, sxh = rep // 2, lax.rem(rep, 2)
    source = device(z=sz, xh=sxh, xl=lax.rem(xh + xl + sxh, 2), y=turn(z, y - sz - HALF))

    barrier = pltpu.get_barrier_semaphore()
    friends = [d for ways in (z_ways, y_ways) for side in ways[0] for d in side]
    friends += [*z_ways[1][0], *z_ways[1][1], y_ways[1][0][0], y_ways[1][1][0]]
    friends += [far_x, near_x, sibling, target, source]
    for friend in friends:
        pl.semaphore_signal(barrier, inc=1, device_id=friend, device_id_type=MESH)
    for load in loads[2:]:
        load.start()
    pl.semaphore_wait(barrier, len(friends))

    links = Links(send_sems, recv_sems)
    fowns, fpairs, gbufs, parts = (fown0, fown1), (fpair0, fpair1), (gbuf0, gbuf1), (part0, part1)
    terms, xterms, prods = (term0, term1), (xterm0, xterm1), (prod0, prod1)
    batch = links.batch(feat)
    first = []
    for h in range(2):
        loads[h].wait()
        first.append(links.send(feat.at[h], fowns[h].at[tz * 2 + txh], target, batch))
    for load in loads[2:]:
        load.wait()

    along = [lax.broadcasted_iota(jnp.int32, (NT, TILE), d) for d in range(2)]

    sections = (core, 1 - core)

    def keys(t):
        name = jnp.zeros((NT, TILE), jnp.int32)
        for i in range(NT):
            name = jnp.where(t == i, ids[0, sections[i // SLOTS], i % SLOTS], name)
        second = t >= SLOTS
        live = t < jnp.where(second, counts[0, sections[1]] + SLOTS, counts[0, sections[0]])
        by_row = jnp.where(live, lax.shift_right_logical(name, 4), -1 - t)
        by_column = jnp.where(live, (name & (Q - 1)) + jnp.where(second, Q, 0), -1 - t)
        return by_row, by_column

    def latest(which):
        t = jnp.max(jnp.where(which, along[0], -1), axis=0, keepdims=True)
        return jnp.where(t < 0, NT, t)

    table_row = lax.broadcasted_iota(jnp.int32, (8, TILE), 0)
    found = jnp.zeros((8, TILE), jnp.int32)
    for i, (down_key, across_key) in enumerate(zip(keys(along[0]), keys(along[1]))):
        before = latest((down_key == across_key) & (along[0] < along[1]))
        found = jnp.where(table_row == 2 * i, before, found)
        found = jnp.where(table_row == 2 * i + 1, latest(down_key == along[1]), found)
    table[...] = found
    chained = pltpu.make_async_copy(table, chains, local_sems.at[7])
    chained.start()

    def transpose(part):
        @pl.loop(0, SLOTS, unroll=4)
        def _(i):
            adj_t[part * SLOTS + i] = adj[0, sections[part], i].T

    def share(h):
        end = links.arrival()
        batch = links.batch(fowns[h])

        def arrived(p):
            chunk = pl.ds(p * 2, 2)
            links.send(fowns[h].at[chunk], fpairs[h].at[chunk], sibling, batch, end)

        def run():
            first[h].wait_recv()
            yield from gather_ring(links, fowns[h], z, xh, z_ways, far_x, True, arrived)
            await_bytes(fpairs[h], end)
            yield

        return run()

    def forward(h):
        for part, buf in enumerate((fowns[h], fpairs[h])):
            sec = sections[part]

            @pl.loop(0, SLOTS, unroll=16)
            def _(i):
                t = part * SLOTS + i
                column = lax.rem(ids[0, sec, i], Q)
                ez, exh = entry(sz, sxh, column // N, lax.rem(column, N))
                value = jnp.dot(adj[0, sec, i], buf[ez * 2 + exh], preferred_element_type=F32)
                prods[h][t] = value + prods[h][chains[0, t]]

            yield

    def backward(h):
        for part in range(2):

            @pl.loop(0, SLOTS, unroll=16)
            def _(i):
                t = part * SLOTS + i
                tile_row = lax.div(ids[0, sections[part], i], Q)
                slot = lax.rem(tile_row, N) * 2 + lax.div(tile_row, N)
                value = jnp.dot(adj_t[t], gbufs[h][slot], preferred_element_type=F32)
                prods[h][t] = value + prods[h][chains[2, t]]

            yield

    def pair_terms(h):
        batch = links.batch(xterms[h])
        ends = [links.arrival() for _ in range(5)]
        for off in OFFSETS:
            zz = turn(z, off)
            for s in range(2):
                for sec in range(2):
                    value = prods[h][chains[3, lax.rem(sec + core, 2) * Q + zz * 2 + s]].astype(BF16)
                    for half in range(2):
                        terms[h][half, zz * 2 + s, pl.ds(sec * 64, 64)] = value[half * 64 : half * 64 + 64]
            chunk = pl.ds(zz * 2, 2)
            links.send(terms[h].at[1 - core, chunk], xterms[h].at[chunk], sibling, batch, ends[min(off, N - off)])
        return ends

    for prod in prods:
        prod[NT] = jnp.zeros((TILE, TILE), F32)
    share0, share1 = share(0), share(1)
    step(share0)
    transpose(0)
    step(share1)
    transpose(1)
    chained.wait()
    for _ in range(2):
        step(share0)
        step(share1)
    step(share0)

    def sum_parts(h, slots, last):
        def fin(value):
            agg[h] = value.astype(BF16)

        def prep(p):
            for s in range(2):
                parts[h][p * 2 + s] = prods[h][chains[1, s * N + p]].astype(BF16)

        return scatter_ring(links, parts[h], prep, slots, last, y, xl, y_ways, near_x, fin)

    forward0, forward1 = forward(0), forward(1)
    step(forward0)
    drain(share0)
    drain(forward0)
    sum0 = sum_parts(0, fslots0, flast0)
    step(sum0)
    step(share1)
    step(forward1)
    drain(share1)
    drain(forward1)
    sum1 = sum_parts(1, fslots1, flast1)
    for _ in range(2):
        step(sum1)
        step(sum0)
    step(sum1)
    drain(sum0)

    pre = jnp.dot(agg[0], weight[pl.ds(0, TILE)], preferred_element_type=F32)
    drain(sum1)
    pre = pre + jnp.dot(agg[1], weight[pl.ds(TILE, TILE)], preferred_element_type=F32)
    gate = jax.nn.sigmoid(pre)
    act_out[...] = (pre * gate).astype(BF16)
    gpre[...] = (gout[...].astype(F32) * gate * (1.0 + pre * (1.0 - gate))).astype(BF16)
    own = y * 2 + xl
    grads = []
    for h in range(2):
        gbufs[h][own] = lax.dot_general(
            gpre[...], weight[pl.ds(h * TILE, TILE)], (((1,), (1,)), ((), ())), preferred_element_type=F32
        ).astype(BF16)
        grads.append(gather_ring(links, gbufs[h], y, xl, y_ways, near_x))
        step(grads[h])

    gpre_t = gpre[...].T
    rows = 2 * TILE // Q
    for h in range(2):
        value = jnp.dot(gpre_t, agg[h], preferred_element_type=F32).astype(BF16)
        for p in range(Q):
            wt[h, (p % N) * 2 + p // N] = value[p * rows : (p + 1) * rows]

    def weight_gradient():
        pair = links.send(wt.at[1 - core], wpair, sibling, links.batch(wpair))
        yield
        pair.wait_recv()
        for q in range(Q):
            wt[core, q] = (wt[core, q].astype(F32) + wpair[q].astype(F32)).astype(BF16)

        def fin(value):
            wgather[place] = value.astype(BF16)

        ring = scatter_ring(links, wt.at[core], lambda p: None, wslots, wlast, y, xl, y_ways, near_x, fin)
        for _ in range(3):
            step(ring)
            yield
        drain(ring)
        ring = gather_ring(links, wgather, z, xh, z_ways, far_x)
        for _ in range(3):
            step(ring)
            yield
        drain(ring)
        value = wgather[0].astype(F32)
        for q in range(1, Q):
            value = value + wgather[q].astype(F32)
        wsum[core] = value
        half = wsum.at[core]
        pair = links.send(half, half, sibling, links.batch(half))
        yield
        pair.wait_recv()
        for h in range(2):
            gw_out[:, pl.ds(h * TILE, TILE)] = wsum[h]
        yield

    wgrad = weight_gradient()
    step(wgrad)
    step(grads[0])
    step(wgrad)
    step(grads[1])
    step(grads[0])
    step(grads[1])
    step(wgrad)
    step(grads[0])
    backward0, backward1 = backward(0), backward(1)
    drain(backward0)

    def sum_terms(h, ends, slots, last):
        order = iter(OFFSETS)

        def prep(p):
            off = next(order)
            if off <= HALF:
                await_bytes(xterms[h].at[pl.ds(0, 2 if off in (0, HALF) else 4)], ends[off])
            for s in range(2):
                value = terms[h][core, p * 2 + s].astype(F32) + xterms[h][p * 2 + s].astype(F32)
                terms[h][core, p * 2 + s] = value.astype(BF16)

        def fin(value):
            for sec in range(2):
                gf_out[sec, :, pl.ds(h * TILE, TILE)] = value[sec * 64 : sec * 64 + 64]

        return scatter_ring(links, terms[h].at[core], prep, slots, last, z, xh, z_ways, far_x, fin)

    out0 = sum_terms(0, pair_terms(0), bslots0, blast0)
    step(wgrad)
    step(out0)
    drain(grads[1])
    drain(backward1)
    step(wgrad)
    out1 = sum_terms(1, pair_terms(1), bslots1, blast1)
    step(out0)
    step(out1)
    step(wgrad)
    step(out0)
    step(out1)
    step(wgrad)
    drain(out0)
    step(out1)
    step(wgrad)
    drain(out1)
    drain(wgrad)
    links.finish()


def store(*refs):
    copies = [pltpu.make_async_copy(refs[i], refs[3 + i], refs[6].at[i]) for i in range(3)]
    for copy in copies:
        copy.start()
    for copy in copies:
        copy.wait()


def shards(features, adjacency, tile_ids, tile_counts, weight, grad_out):
    block = (TILE, TILE)
    hbm = pl.BlockSpec(memory_space=pltpu.HBM)
    vmem = pl.BlockSpec(memory_space=pltpu.VMEM)
    rows = 2 * TILE // Q
    stripe, part = (rows, 2 * TILE), (rows, TILE)
    slots, last = (2, 5), (5,)
    activated, grad_weight, grad_features = pl.pallas_call(
        kernel,
        out_shape=(
            pltpu.VMEM((TILE, 2 * TILE), BF16),
            pltpu.VMEM(stripe, F32),
            pltpu.VMEM((2, 64, 2 * TILE), F32),
        ),
        in_specs=[hbm] * 6,
        out_specs=(vmem, vmem, vmem),
        scratch_shapes=[
            pltpu.VMEM((2,) + block, BF16),
            pltpu.VMEM((1, 2, SLOTS) + block, BF16),
            pltpu.VMEM((2 * TILE, 2 * TILE), BF16),
            pltpu.VMEM((TILE, 2 * TILE), BF16),
            *[pltpu.VMEM((Q,) + block, BF16)] * 4,
            *[pltpu.VMEM((Q,) + block, BF16)] * 2,
            *[pltpu.VMEM((Q,) + block, BF16)] * 2,
            *[pltpu.VMEM((2, Q) + block, BF16)] * 2,
            *[pltpu.VMEM((Q,) + block, BF16)] * 2,
            pltpu.VMEM((NT,) + block, BF16),
            *[pltpu.VMEM((NT + 1,) + block, F32)] * 2,
            pltpu.VMEM((2,) + block, BF16),
            pltpu.VMEM((TILE, 2 * TILE), BF16),
            *[pltpu.VMEM(slots + block, BF16)] * 2,
            *[pltpu.VMEM(last + block, BF16)] * 2,
            *[pltpu.VMEM(slots + block, BF16)] * 2,
            *[pltpu.VMEM(last + block, BF16)] * 2,
            pltpu.VMEM((2, Q) + part, BF16),
            pltpu.VMEM((Q,) + part, BF16),
            pltpu.VMEM(slots + part, BF16),
            pltpu.VMEM(last + part, BF16),
            pltpu.VMEM((2,) + part, F32),
            pltpu.VMEM((Q,) + part, BF16),
            pltpu.SMEM((1, 2, SLOTS), jnp.int32),
            pltpu.SMEM((1, 2), jnp.int32),
            pltpu.VMEM((8, TILE), jnp.int32),
            pltpu.SMEM((8, TILE), jnp.int32),
            pltpu.SemaphoreType.DMA((8,)),
            pltpu.SemaphoreType.DMA((N_SEND,)),
            pltpu.SemaphoreType.DMA((N_RECV,)),
        ],
        compiler_params=pltpu.CompilerParams(
            collective_id=0, has_side_effects=True, vmem_limit_bytes=40 * 1024 * 1024
        ),
    )(*[pltpu.with_memory_space_constraint(x, pltpu.HBM) for x in (features, adjacency, tile_ids, tile_counts, weight, grad_out)])
    results = (activated, grad_weight, grad_features)
    activated, grad_weight, grad_features = pl.pallas_call(
        store,
        out_shape=[pltpu.HBM(x.shape, x.dtype) for x in results],
        in_specs=[vmem] * 3,
        out_specs=[hbm] * 3,
        scratch_shapes=[pltpu.SemaphoreType.DMA((3,))],
    )(*[pltpu.with_memory_space_constraint(x, pltpu.VMEM) for x in results])
    return activated, grad_weight.T, grad_features


def solution(mesh):
    return jax.shard_map(
        shards,
        mesh=mesh,
        in_specs=(
            P(("rows", "rep"), None),
            P("rows", "rep", None, None, None),
            P("rows", "rep", None),
            P("rows", "rep"),
            P(),
            P(("rows", "rep"), None),
        ),
        out_specs=(P(("rows", "rep"), None), P(None, "rep"), P("rep", "rows", None)),
        check_vma=False,
    )
```

```python
import jax
import jax.numpy as jnp
from jax import lax
from jax.experimental import pallas as pl
from jax.experimental.pallas import tpu as pltpu
from jax.sharding import PartitionSpec as P

N = 8
Q = 2 * N
HALF = N // 2
TILE = 128
SLOTS = 16
NT = 2 * SLOTS
OFFSETS = (4, 3, 5, 2, 6, 1, 7, 0)
F32 = jnp.float32
BF16 = jnp.bfloat16
MESH = pl.DeviceIdType.MESH
N_SEND = 17
N_RECV = 83


class Links:
    def __init__(self, send_sems, recv_sems):
        self.send_sems, self.recv_sems, self.n_send, self.n_recv = send_sems, recv_sems, 0, 0
        self.finishing = []

    def batch(self, everything):
        sem = self.send_sems.at[self.n_send]
        self.n_send += 1
        assert self.n_send <= N_SEND
        self.finishing.append((everything, sem))
        return sem

    def arrival(self):
        sem = self.recv_sems.at[self.n_recv]
        self.n_recv += 1
        assert self.n_recv <= N_RECV
        return sem

    def send(self, src, dst, device, batch, arrival=None):
        copy = pltpu.make_async_remote_copy(
            src_ref=src,
            dst_ref=dst,
            send_sem=batch,
            recv_sem=self.arrival() if arrival is None else arrival,
            device_id=device,
            device_id_type=MESH,
        )
        copy.start()
        return copy

    def finish(self):
        for everything, sem in self.finishing:
            await_bytes(everything, sem)


def await_bytes(ref, sem):
    pltpu.make_async_copy(ref, ref, sem).wait()


def gather_ring(links, buf, pos, sub, ways, partner, straight=False, arrived=None):
    own, two_blocks = buf.at[pos * 2 + sub], buf.at[pl.ds(0, 2)]
    batch = links.batch(buf.at[pl.ds(0, Q - 1)])
    came = [[links.arrival() for _ in range(2)] for _ in range(3)]
    four, pair = links.arrival(), links.arrival()

    def position(side, distance):
        return lax.rem(pos + (N - distance, distance)[side], N)

    for distance in (2, 1) if straight else (1,):
        for t in (1, 0):
            for side in range(2):
                links.send(own, own, ways[distance - 1][side][t], batch, came[distance - 1][side])
    links.send(own, own, partner, batch, pair)
    yield

    def first():
        for side in range(2):
            p = position(side, 1)
            await_bytes(two_blocks, came[0][side])
            if not straight:
                chunk = buf.at[pl.ds(p * 2, 2)]
                links.send(chunk, chunk, ways[0][side][0], batch, came[1][side])
        if arrived:
            for side in range(2):
                arrived(position(side, 1))

    if not straight:
        first()
        yield
    for side in range(2):
        p = position(side, 2)
        await_bytes(two_blocks, came[1][side])
        block, chunk = buf.at[p * 2 + (sub if side == 0 else 1 - sub)], buf.at[pl.ds(p * 2, 2)]
        links.send(block, block, ways[1][side][0], batch, four)
        links.send(chunk, chunk, ways[0][side][0], batch, came[2][side])
    if arrived:
        for side in range(2):
            arrived(position(side, 2))
    if straight:
        yield
        first()
    await_bytes(own, pair)
    if arrived:
        arrived(pos)
    yield
    for side in range(2):
        await_bytes(two_blocks, came[2][side])
        if arrived:
            arrived(position(side, 3))
    await_bytes(two_blocks, four)
    if arrived:
        arrived(position(0, HALF))
    yield


def scatter_ring(links, own, prep, slots, last, pos, sub, ways, partner, done):
    batch, end = links.batch(own.at[pl.ds(0, Q - 1)]), links.arrival()
    at_two, at_one = [links.arrival() for _ in range(2)], [links.arrival() for _ in range(2)]

    def at(side, distance):
        return lax.rem(pos + (distance, N - distance)[side], N)

    p = at(0, HALF)
    prep(p)
    for side in range(2):
        links.send(own.at[p * 2 + side], slots.at[side, 2], ways[1][side][0], batch, at_two[side])
    for side in range(2):
        p = at(side, 3)
        prep(p)
        links.send(own.at[pl.ds(p * 2, 2)], slots.at[side, pl.ds(0, 2)], ways[0][side][0], batch, at_two[side])
    yield
    for side in range(2):
        p = at(side, 2)
        prep(p)
        await_bytes(slots.at[side, pl.ds(0, 3)], at_two[side])
        for s in range(2):
            value = slots[side, s].astype(F32) + own[p * 2 + s].astype(F32)
            if s == side:
                value = value + slots[side, 2].astype(F32)
            slots[side, s] = value.astype(BF16)
        links.send(slots.at[side, pl.ds(0, 2)], slots.at[side, pl.ds(3, 2)], ways[0][side][0], batch, at_one[side])
    yield
    for side in range(2):
        p = at(side, 1)
        prep(p)
        await_bytes(slots.at[side, pl.ds(3, 2)], at_one[side])
        for s in range(2):
            slots[side, 3 + s] = (slots[side, 3 + s].astype(F32) + own[p * 2 + s].astype(F32)).astype(BF16)
        for t in (1, 0):
            block = slots.at[side, 3 + (sub if t == 0 else 1 - sub)]
            links.send(block, last.at[side * 2 + t], ways[0][side][t], batch, end)
    prep(pos)
    links.send(own.at[pos * 2 + 1 - sub], last.at[4], partner, batch, end)
    yield
    await_bytes(last, end)
    value = own[pos * 2 + sub].astype(F32)
    for i in range(5):
        value = value + last[i].astype(F32)
    done(value)
    yield


def drain(*parts):
    parts = list(parts)
    while parts:
        for part in list(parts):
            if next(part, "end") == "end":
                parts.remove(part)


def step(part, count=1):
    for _ in range(count):
        next(part, None)


def kernel(
    feat_in, adj_in, ids_in, counts_in, weight_in, gout_in,
    act_out, gw_out, gf_out,
    feat, adj, weight, gout, fown0, fown1, fpair0, fpair1, gbuf0, gbuf1, part0, part1, term0, term1, xterm0, xterm1, adj_t, prod0, prod1, agg, gpre,
    fslots0, fslots1, flast0, flast1, bslots0, bslots1, blast0, blast1,
    wt, wpair, wslots, wlast, wsum, wgather,
    ids, counts, table, chains, local_sems, send_sems, recv_sems,
):
    row, rep = lax.axis_index("rows"), lax.axis_index("rep")
    z, xh, core = row // 4, lax.rem(row // 2, 2), lax.rem(row, 2)
    xl, y = rep // N, lax.rem(rep, N)
    place = z * 2 + xh

    loads = [
        pltpu.make_async_copy(src, dst, local_sems.at[i])
        for i, (src, dst) in enumerate(
            [(feat_in.at[:, pl.ds(h * TILE, TILE)], feat.at[h]) for h in range(2)]
            + [(ids_in, ids), (counts_in, counts), (adj_in, adj), (weight_in, weight), (gout_in, gout)]
        )
    ]
    for load in loads[:2]:
        load.start()

    def device(z=z, xh=xh, core=core, xl=xl, y=y):
        return {"rows": (z * 2 + xh) * 2 + core, "rep": xl * N + y}

    def turn(value, by):
        return lax.rem(value + by + 2 * N, N)

    z_ways, y_ways = [], []
    for by in (1, 2):
        z_ways.append([(device(z=t), device(z=t, xh=1 - xh)) for t in (turn(z, by), turn(z, -by))])
        y_ways.append([(device(y=t), device(y=t, xl=1 - xl)) for t in (turn(y, by), turn(y, -by))])
    far_x, near_x, sibling = device(xh=1 - xh), device(xl=1 - xl), device(core=1 - core)

    def entry(z, xh, xl, y):
        home = z * 2 + xh
        return turn(z, y - lax.rem(home, N) + HALF), lax.rem(xl + home // N + xh, 2)

    tz, txh = entry(z, xh, xl, y)
    target = device(z=tz, xh=txh, xl=place // N, y=lax.rem(place, N))
    sz, sxh = rep // 2, lax.rem(rep, 2)
    source = device(z=sz, xh=sxh, xl=lax.rem(xh + xl + sxh, 2), y=turn(z, y - sz - HALF))

    barrier = pltpu.get_barrier_semaphore()
    friends = [source, target]
    friends += [d for ways in (z_ways, y_ways) for side in ways[0] for d in side]
    friends += [*z_ways[1][0], *z_ways[1][1], y_ways[1][0][0], y_ways[1][1][0]]
    friends += [far_x, near_x, sibling]
    for friend in friends:
        pl.semaphore_signal(barrier, inc=1, device_id=friend, device_id_type=MESH)
    for load in loads[2:]:
        load.start()
    pl.semaphore_wait(barrier, len(friends))

    links = Links(send_sems, recv_sems)
    fowns, fpairs, gbufs, parts = (fown0, fown1), (fpair0, fpair1), (gbuf0, gbuf1), (part0, part1)
    terms, xterms, prods = (term0, term1), (xterm0, xterm1), (prod0, prod1)
    batch = links.batch(feat)
    first = []
    for h in range(2):
        loads[h].wait()
        first.append(links.send(feat.at[h], fowns[h].at[tz * 2 + txh], target, batch))
    for load in loads[2:]:
        load.wait()

    along = [lax.broadcasted_iota(jnp.int32, (NT, TILE), d) for d in range(2)]

    sections = (core, 1 - core)

    def keys(t):
        name = jnp.zeros((NT, TILE), jnp.int32)
        for i in range(NT):
            name = jnp.where(t == i, ids[0, sections[i // SLOTS], i % SLOTS], name)
        second = t >= SLOTS
        live = t < jnp.where(second, counts[0, sections[1]] + SLOTS, counts[0, sections[0]])
        by_row = jnp.where(live, lax.shift_right_logical(name, 4), -1 - t)
        by_column = jnp.where(live, (name & (Q - 1)) + jnp.where(second, Q, 0), -1 - t)
        return by_row, by_column

    def latest(which):
        t = jnp.max(jnp.where(which, along[0], -1), axis=0, keepdims=True)
        return jnp.where(t < 0, NT, t)

    table_row = lax.broadcasted_iota(jnp.int32, (8, TILE), 0)
    found = jnp.zeros((8, TILE), jnp.int32)
    for i, (down_key, across_key) in enumerate(zip(keys(along[0]), keys(along[1]))):
        before = latest((down_key == across_key) & (along[0] < along[1]))
        found = jnp.where(table_row == 2 * i, before, found)
        found = jnp.where(table_row == 2 * i + 1, latest(down_key == along[1]), found)
    table[...] = found
    chained = pltpu.make_async_copy(table, chains, local_sems.at[7])
    chained.start()

    def transpose(part):
        @pl.loop(0, SLOTS, unroll=16)
        def _(i):
            adj_t[part * SLOTS + i] = adj[0, sections[part], i].T

    def share(h):
        end = links.arrival()
        batch = links.batch(fowns[h])

        def arrived(p):
            chunk = pl.ds(p * 2, 2)
            links.send(fowns[h].at[chunk], fpairs[h].at[chunk], sibling, batch, end)

        def run():
            first[h].wait_recv()
            yield from gather_ring(links, fowns[h], z, xh, z_ways, far_x, True, arrived)
            await_bytes(fpairs[h], end)
            yield

        return run()

    def forward(h):
        for part, buf in enumerate((fowns[h], fpairs[h])):
            sec = sections[part]

            @pl.loop(0, SLOTS, unroll=16)
            def _(i):
                t = part * SLOTS + i
                column = lax.rem(ids[0, sec, i], Q)
                ez, exh = entry(sz, sxh, column // N, lax.rem(column, N))
                value = jnp.dot(adj[0, sec, i], buf[ez * 2 + exh], preferred_element_type=F32)
                prods[h][t] = value + prods[h][chains[0, t]]

            yield

    def backward(h):
        for part in range(2):

            @pl.loop(0, SLOTS, unroll=16)
            def _(i):
                t = part * SLOTS + i
                tile_row = lax.div(ids[0, sections[part], i], Q)
                slot = lax.rem(tile_row, N) * 2 + lax.div(tile_row, N)
                value = jnp.dot(adj_t[t], gbufs[h][slot], preferred_element_type=F32)
                prods[h][t] = value + prods[h][chains[2, t]]

            yield

    def pair_terms(h):
        batch = links.batch(xterms[h])
        ends = [links.arrival() for _ in range(5)]
        for off in OFFSETS:
            zz = turn(z, off)
            for s in range(2):
                for sec in range(2):
                    value = prods[h][chains[3, lax.rem(sec + core, 2) * Q + zz * 2 + s]].astype(BF16)
                    for half in range(2):
                        terms[h][half, zz * 2 + s, pl.ds(sec * 64, 64)] = value[half * 64 : half * 64 + 64]
            chunk = pl.ds(zz * 2, 2)
            links.send(terms[h].at[1 - core, chunk], xterms[h].at[chunk], sibling, batch, ends[min(off, N - off)])
        return ends

    for prod in prods:
        prod[NT] = jnp.zeros((TILE, TILE), F32)
    share0, share1 = share(0), share(1)
    step(share0)
    transpose(0)
    step(share1)
    transpose(1)
    chained.wait()
    for _ in range(2):
        step(share0)
        step(share1)
    step(share0)

    def sum_parts(h, slots, last):
        def fin(value):
            agg[h] = value.astype(BF16)

        def prep(p):
            for s in range(2):
                parts[h][p * 2 + s] = prods[h][chains[1, s * N + p]].astype(BF16)

        return scatter_ring(links, parts[h], prep, slots, last, y, xl, y_ways, near_x, fin)

    forward0, forward1 = forward(0), forward(1)
    step(forward0)
    drain(share0)
    drain(forward0)
    sum0 = sum_parts(0, fslots0, flast0)
    step(sum0)
    step(share1)
    step(forward1)
    drain(share1)
    drain(forward1)
    sum1 = sum_parts(1, fslots1, flast1)
    for _ in range(2):
        step(sum1)
        step(sum0)
    step(sum1)
    drain(sum0)

    pre = jnp.dot(agg[0], weight[pl.ds(0, TILE)], preferred_element_type=F32)
    drain(sum1)
    pre = pre + jnp.dot(agg[1], weight[pl.ds(TILE, TILE)], preferred_element_type=F32)
    gate = jax.nn.sigmoid(pre)
    act_out[...] = (pre * gate).astype(BF16)
    gpre[...] = (gout[...].astype(F32) * gate * (1.0 + pre * (1.0 - gate))).astype(BF16)
    own = y * 2 + xl
    grads = []
    for h in range(2):
        gbufs[h][own] = lax.dot_general(
            gpre[...], weight[pl.ds(h * TILE, TILE)], (((1,), (1,)), ((), ())), preferred_element_type=F32
        ).astype(BF16)
        grads.append(gather_ring(links, gbufs[h], y, xl, y_ways, near_x))
        step(grads[h])

    gpre_t = gpre[...].T
    rows = 2 * TILE // Q
    for h in range(2):
        value = jnp.dot(gpre_t, agg[h], preferred_element_type=F32).astype(BF16)
        for p in range(Q):
            wt[h, (p % N) * 2 + p // N] = value[p * rows : (p + 1) * rows]

    def weight_gradient():
        pair = links.send(wt.at[1 - core], wpair, sibling, links.batch(wpair))
        yield
        pair.wait_recv()
        for q in range(Q):
            wt[core, q] = (wt[core, q].astype(F32) + wpair[q].astype(F32)).astype(BF16)

        def fin(value):
            wgather[place] = value.astype(BF16)

        ring = scatter_ring(links, wt.at[core], lambda p: None, wslots, wlast, y, xl, y_ways, near_x, fin)
        for _ in range(3):
            step(ring)
            yield
        drain(ring)
        ring = gather_ring(links, wgather, z, xh, z_ways, far_x)
        for _ in range(3):
            step(ring)
            yield
        drain(ring)
        value = wgather[0].astype(F32)
        for q in range(1, Q):
            value = value + wgather[q].astype(F32)
        wsum[core] = value
        half = wsum.at[core]
        pair = links.send(half, half, sibling, links.batch(half))
        yield
        pair.wait_recv()
        for h in range(2):
            gw_out[:, pl.ds(h * TILE, TILE)] = wsum[h]
        yield

    wgrad = weight_gradient()
    step(wgrad)
    step(grads[0])
    step(wgrad)
    step(grads[1])
    step(grads[0])
    step(grads[1])
    step(wgrad)
    step(grads[0])
    backward0, backward1 = backward(0), backward(1)
    drain(backward0)

    def sum_terms(h, ends, slots, last):
        order = iter(OFFSETS)

        def prep(p):
            off = next(order)
            if off <= HALF:
                await_bytes(xterms[h].at[pl.ds(0, 2 if off in (0, HALF) else 4)], ends[off])
            for s in range(2):
                value = terms[h][core, p * 2 + s].astype(F32) + xterms[h][p * 2 + s].astype(F32)
                terms[h][core, p * 2 + s] = value.astype(BF16)

        def fin(value):
            for sec in range(2):
                gf_out[sec, :, pl.ds(h * TILE, TILE)] = value[sec * 64 : sec * 64 + 64]

        return scatter_ring(links, terms[h].at[core], prep, slots, last, z, xh, z_ways, far_x, fin)

    out0 = sum_terms(0, pair_terms(0), bslots0, blast0)
    step(out0)
    drain(grads[1])
    drain(backward1)
    step(wgrad, 2)
    out1 = sum_terms(1, pair_terms(1), bslots1, blast1)
    step(out0)
    step(out1)
    step(wgrad)
    step(out0)
    step(out1)
    step(wgrad)
    drain(out0)
    step(out1)
    step(wgrad)
    drain(out1)
    drain(wgrad)
    links.finish()


def store(*refs):
    copies = [pltpu.make_async_copy(refs[i], refs[3 + i], refs[6].at[i]) for i in range(3)]
    for copy in copies:
        copy.start()
    for copy in copies:
        copy.wait()


def shards(features, adjacency, tile_ids, tile_counts, weight, grad_out):
    block = (TILE, TILE)
    hbm = pl.BlockSpec(memory_space=pltpu.HBM)
    vmem = pl.BlockSpec(memory_space=pltpu.VMEM)
    rows = 2 * TILE // Q
    stripe, part = (rows, 2 * TILE), (rows, TILE)
    slots, last = (2, 5), (5,)
    activated, grad_weight, grad_features = pl.pallas_call(
        kernel,
        out_shape=(
            pltpu.VMEM((TILE, 2 * TILE), BF16),
            pltpu.VMEM(stripe, F32),
            pltpu.VMEM((2, 64, 2 * TILE), F32),
        ),
        in_specs=[hbm] * 6,
        out_specs=(vmem, vmem, vmem),
        scratch_shapes=[
            pltpu.VMEM((2,) + block, BF16),
            pltpu.VMEM((1, 2, SLOTS) + block, BF16),
            pltpu.VMEM((2 * TILE, 2 * TILE), BF16),
            pltpu.VMEM((TILE, 2 * TILE), BF16),
            *[pltpu.VMEM((Q,) + block, BF16)] * 4,
            *[pltpu.VMEM((Q,) + block, BF16)] * 2,
            *[pltpu.VMEM((Q,) + block, BF16)] * 2,
            *[pltpu.VMEM((2, Q) + block, BF16)] * 2,
            *[pltpu.VMEM((Q,) + block, BF16)] * 2,
            pltpu.VMEM((NT,) + block, BF16),
            *[pltpu.VMEM((NT + 1,) + block, F32)] * 2,
            pltpu.VMEM((2,) + block, BF16),
            pltpu.VMEM((TILE, 2 * TILE), BF16),
            *[pltpu.VMEM(slots + block, BF16)] * 2,
            *[pltpu.VMEM(last + block, BF16)] * 2,
            *[pltpu.VMEM(slots + block, BF16)] * 2,
            *[pltpu.VMEM(last + block, BF16)] * 2,
            pltpu.VMEM((2, Q) + part, BF16),
            pltpu.VMEM((Q,) + part, BF16),
            pltpu.VMEM(slots + part, BF16),
            pltpu.VMEM(last + part, BF16),
            pltpu.VMEM((2,) + part, F32),
            pltpu.VMEM((Q,) + part, BF16),
            pltpu.SMEM((1, 2, SLOTS), jnp.int32),
            pltpu.SMEM((1, 2), jnp.int32),
            pltpu.VMEM((8, TILE), jnp.int32),
            pltpu.SMEM((8, TILE), jnp.int32),
            pltpu.SemaphoreType.DMA((8,)),
            pltpu.SemaphoreType.DMA((N_SEND,)),
            pltpu.SemaphoreType.DMA((N_RECV,)),
        ],
        compiler_params=pltpu.CompilerParams(
            collective_id=0, has_side_effects=True, vmem_limit_bytes=40 * 1024 * 1024
        ),
    )(*[pltpu.with_memory_space_constraint(x, pltpu.HBM) for x in (features, adjacency, tile_ids, tile_counts, weight, grad_out)])
    results = (activated, grad_weight, grad_features)
    activated, grad_weight, grad_features = pl.pallas_call(
        store,
        out_shape=[pltpu.HBM(x.shape, x.dtype) for x in results],
        in_specs=[vmem] * 3,
        out_specs=[hbm] * 3,
        scratch_shapes=[pltpu.SemaphoreType.DMA((3,))],
    )(*[pltpu.with_memory_space_constraint(x, pltpu.VMEM) for x in results])
    return activated, grad_weight.T, grad_features


def solution(mesh):
    return jax.shard_map(
        shards,
        mesh=mesh,
        in_specs=(
            P(("rows", "rep"), None),
            P("rows", "rep", None, None, None),
            P("rows", "rep", None),
            P("rows", "rep"),
            P(),
            P(("rows", "rep"), None),
        ),
        out_specs=(P(("rows", "rep"), None), P(None, "rep"), P("rep", "rows", None)),
        check_vma=False,
    )
```

```python
import jax
import jax.numpy as jnp
from jax import lax
from jax.experimental import pallas as pl
from jax.experimental.pallas import tpu as pltpu
from jax.sharding import PartitionSpec as P

N = 8
Q = 2 * N
HALF = N // 2
TILE = 128
SLOTS = 16
NT = 2 * SLOTS
OFFSETS = (4, 3, 5, 2, 6, 1, 7, 0)
F32 = jnp.float32
BF16 = jnp.bfloat16
MESH = pl.DeviceIdType.MESH
N_SEND = 17
N_RECV = 83


class Links:
    def __init__(self, send_sems, recv_sems):
        self.send_sems, self.recv_sems, self.n_send, self.n_recv = send_sems, recv_sems, 0, 0
        self.finishing = []

    def batch(self, everything):
        sem = self.send_sems.at[self.n_send]
        self.n_send += 1
        assert self.n_send <= N_SEND
        self.finishing.append((everything, sem))
        return sem

    def arrival(self):
        sem = self.recv_sems.at[self.n_recv]
        self.n_recv += 1
        assert self.n_recv <= N_RECV
        return sem

    def send(self, src, dst, device, batch, arrival=None):
        copy = pltpu.make_async_remote_copy(
            src_ref=src,
            dst_ref=dst,
            send_sem=batch,
            recv_sem=self.arrival() if arrival is None else arrival,
            device_id=device,
            device_id_type=MESH,
        )
        copy.start()
        return copy

    def finish(self):
        for everything, sem in self.finishing:
            await_bytes(everything, sem)


def await_bytes(ref, sem):
    pltpu.make_async_copy(ref, ref, sem).wait()


def gather_ring(links, buf, pos, sub, ways, partner, straight=False, arrived=None):
    own, two_blocks = buf.at[pos * 2 + sub], buf.at[pl.ds(0, 2)]
    batch = links.batch(buf.at[pl.ds(0, Q - 1)])
    came = [[links.arrival() for _ in range(2)] for _ in range(3)]
    four, pair = links.arrival(), links.arrival()

    def position(side, distance):
        return lax.rem(pos + (N - distance, distance)[side], N)

    for distance in (2, 1) if straight else (1,):
        for t in (1, 0):
            for side in range(2):
                links.send(own, own, ways[distance - 1][side][t], batch, came[distance - 1][side])
    links.send(own, own, partner, batch, pair)
    yield

    def first():
        for side in range(2):
            p = position(side, 1)
            await_bytes(two_blocks, came[0][side])
            if not straight:
                chunk = buf.at[pl.ds(p * 2, 2)]
                links.send(chunk, chunk, ways[0][side][0], batch, came[1][side])
        if arrived:
            for side in range(2):
                arrived(position(side, 1))

    if not straight:
        first()
        yield
    for side in range(2):
        p = position(side, 2)
        await_bytes(two_blocks, came[1][side])
        block, chunk = buf.at[p * 2 + (sub if side == 0 else 1 - sub)], buf.at[pl.ds(p * 2, 2)]
        links.send(block, block, ways[1][side][0], batch, four)
        links.send(chunk, chunk, ways[0][side][0], batch, came[2][side])
    if arrived:
        for side in range(2):
            arrived(position(side, 2))
    if straight:
        yield
        first()
    await_bytes(own, pair)
    if arrived:
        arrived(pos)
    yield
    for side in range(2):
        await_bytes(two_blocks, came[2][side])
        if arrived:
            arrived(position(side, 3))
    await_bytes(two_blocks, four)
    if arrived:
        arrived(position(0, HALF))
    yield


def scatter_ring(links, own, prep, slots, last, pos, sub, ways, partner, done):
    batch, end = links.batch(own.at[pl.ds(0, Q - 1)]), links.arrival()
    at_two, at_one = [links.arrival() for _ in range(2)], [links.arrival() for _ in range(2)]

    def at(side, distance):
        return lax.rem(pos + (distance, N - distance)[side], N)

    p = at(0, HALF)
    prep(p)
    for side in range(2):
        links.send(own.at[p * 2 + side], slots.at[side, 2], ways[1][side][0], batch, at_two[side])
    for side in range(2):
        p = at(side, 3)
        prep(p)
        links.send(own.at[pl.ds(p * 2, 2)], slots.at[side, pl.ds(0, 2)], ways[0][side][0], batch, at_two[side])
    yield
    for side in range(2):
        p = at(side, 2)
        prep(p)
        await_bytes(slots.at[side, pl.ds(0, 3)], at_two[side])
        for s in range(2):
            value = slots[side, s].astype(F32) + own[p * 2 + s].astype(F32)
            if s == side:
                value = value + slots[side, 2].astype(F32)
            slots[side, s] = value.astype(BF16)
        links.send(slots.at[side, pl.ds(0, 2)], slots.at[side, pl.ds(3, 2)], ways[0][side][0], batch, at_one[side])
    yield
    for side in range(2):
        p = at(side, 1)
        prep(p)
        await_bytes(slots.at[side, pl.ds(3, 2)], at_one[side])
        for s in range(2):
            slots[side, 3 + s] = (slots[side, 3 + s].astype(F32) + own[p * 2 + s].astype(F32)).astype(BF16)
        for t in (1, 0):
            block = slots.at[side, 3 + (sub if t == 0 else 1 - sub)]
            links.send(block, last.at[side * 2 + t], ways[0][side][t], batch, end)
    prep(pos)
    links.send(own.at[pos * 2 + 1 - sub], last.at[4], partner, batch, end)
    yield
    await_bytes(last, end)
    value = own[pos * 2 + sub].astype(F32)
    for i in range(5):
        value = value + last[i].astype(F32)
    done(value)
    yield


def drain(*parts):
    parts = list(parts)
    while parts:
        for part in list(parts):
            if next(part, "end") == "end":
                parts.remove(part)


def step(part, count=1):
    for _ in range(count):
        next(part, None)


def kernel(
    feat_in, adj_in, ids_in, counts_in, weight_in, gout_in,
    act_out, gw_out, gf_out,
    feat, adj, weight, weight_t, gout, fown0, fown1, fpair0, fpair1, gbuf0, gbuf1, part0, part1, term0, term1, xterm0, xterm1, adj_t, prod0, prod1, agg, gpre,
    fslots0, fslots1, flast0, flast1, bslots0, bslots1, blast0, blast1,
    wt, wpair, wslots, wlast, wsum, wgather,
    ids, counts, table, chains, local_sems, send_sems, recv_sems,
):
    row, rep = lax.axis_index("rows"), lax.axis_index("rep")
    z, xh, core = row // 4, lax.rem(row // 2, 2), lax.rem(row, 2)
    xl, y = rep // N, lax.rem(rep, N)
    place = z * 2 + xh

    loads = [
        pltpu.make_async_copy(src, dst, local_sems.at[i])
        for i, (src, dst) in enumerate(
            [(feat_in.at[:, pl.ds(h * TILE, TILE)], feat.at[h]) for h in range(2)]
            + [(ids_in, ids), (counts_in, counts), (adj_in, adj), (weight_in, weight), (gout_in, gout)]
        )
    ]
    for load in loads[:2]:
        load.start()

    def device(z=z, xh=xh, core=core, xl=xl, y=y):
        return {"rows": (z * 2 + xh) * 2 + core, "rep": xl * N + y}

    def turn(value, by):
        return lax.rem(value + by + 2 * N, N)

    z_ways, y_ways = [], []
    for by in (1, 2):
        z_ways.append([(device(z=t), device(z=t, xh=1 - xh)) for t in (turn(z, by), turn(z, -by))])
        y_ways.append([(device(y=t), device(y=t, xl=1 - xl)) for t in (turn(y, by), turn(y, -by))])
    far_x, near_x, sibling = device(xh=1 - xh), device(xl=1 - xl), device(core=1 - core)

    def entry(z, xh, xl, y):
        home = z * 2 + xh
        return turn(z, y - lax.rem(home, N) + HALF), lax.rem(xl + home // N + xh, 2)

    tz, txh = entry(z, xh, xl, y)
    target = device(z=tz, xh=txh, xl=place // N, y=lax.rem(place, N))
    sz, sxh = rep // 2, lax.rem(rep, 2)
    source = device(z=sz, xh=sxh, xl=lax.rem(xh + xl + sxh, 2), y=turn(z, y - sz - HALF))

    barrier = pltpu.get_barrier_semaphore()
    friends = [source, target]
    friends += [d for ways in (z_ways, y_ways) for side in ways[0] for d in side]
    friends += [*z_ways[1][0], *z_ways[1][1], y_ways[1][0][0], y_ways[1][1][0]]
    friends += [far_x, near_x, sibling]
    for friend in friends:
        pl.semaphore_signal(barrier, inc=1, device_id=friend, device_id_type=MESH)
    for load in loads[2:]:
        load.start()
    pl.semaphore_wait(barrier, len(friends))

    links = Links(send_sems, recv_sems)
    fowns, fpairs, gbufs, parts = (fown0, fown1), (fpair0, fpair1), (gbuf0, gbuf1), (part0, part1)
    terms, xterms, prods = (term0, term1), (xterm0, xterm1), (prod0, prod1)
    batch = links.batch(feat)
    first = []
    for h in range(2):
        loads[h].wait()
        first.append(links.send(feat.at[h], fowns[h].at[tz * 2 + txh], target, batch))
    for load in loads[2:]:
        load.wait()

    along = [lax.broadcasted_iota(jnp.int32, (NT, TILE), d) for d in range(2)]

    sections = (core, 1 - core)

    def keys(t):
        name = jnp.zeros((NT, TILE), jnp.int32)
        for i in range(NT):
            name = jnp.where(t == i, ids[0, sections[i // SLOTS], i % SLOTS], name)
        second = t >= SLOTS
        live = t < jnp.where(second, counts[0, sections[1]] + SLOTS, counts[0, sections[0]])
        by_row = jnp.where(live, lax.shift_right_logical(name, 4), -1 - t)
        by_column = jnp.where(live, (name & (Q - 1)) + jnp.where(second, Q, 0), -1 - t)
        return by_row, by_column

    def latest(which):
        t = jnp.max(jnp.where(which, along[0], -1), axis=0, keepdims=True)
        return jnp.where(t < 0, NT, t)

    table_row = lax.broadcasted_iota(jnp.int32, (8, TILE), 0)
    found = jnp.zeros((8, TILE), jnp.int32)
    for i, (down_key, across_key) in enumerate(zip(keys(along[0]), keys(along[1]))):
        before = latest((down_key == across_key) & (along[0] < along[1]))
        found = jnp.where(table_row == 2 * i, before, found)
        found = jnp.where(table_row == 2 * i + 1, latest(down_key == along[1]), found)
    table[...] = found
    chained = pltpu.make_async_copy(table, chains, local_sems.at[7])
    chained.start()

    def transpose(part):
        @pl.loop(0, SLOTS, unroll=16)
        def _(i):
            adj_t[part * SLOTS + i] = adj[0, sections[part], i].T

    def share(h):
        end = links.arrival()
        batch = links.batch(fowns[h])

        def arrived(p):
            chunk = pl.ds(p * 2, 2)
            links.send(fowns[h].at[chunk], fpairs[h].at[chunk], sibling, batch, end)

        def run():
            first[h].wait_recv()
            yield from gather_ring(links, fowns[h], z, xh, z_ways, far_x, True, arrived)
            await_bytes(fpairs[h], end)
            yield

        return run()

    def forward(h):
        for part, buf in enumerate((fowns[h], fpairs[h])):
            sec = sections[part]

            @pl.loop(0, SLOTS, unroll=16)
            def _(i):
                t = part * SLOTS + i
                column = lax.rem(ids[0, sec, i], Q)
                ez, exh = entry(sz, sxh, column // N, lax.rem(column, N))
                value = jnp.dot(adj[0, sec, i], buf[ez * 2 + exh], preferred_element_type=F32)
                prods[h][t] = value + prods[h][chains[0, t]]

            yield

    def backward(h):
        for part in range(2):

            @pl.loop(0, SLOTS, unroll=16)
            def _(i):
                t = part * SLOTS + i
                tile_row = lax.div(ids[0, sections[part], i], Q)
                slot = lax.rem(tile_row, N) * 2 + lax.div(tile_row, N)
                value = jnp.dot(adj_t[t], gbufs[h][slot], preferred_element_type=F32)
                prods[h][t] = value + prods[h][chains[2, t]]

            yield

    def pair_terms(h):
        batch = links.batch(xterms[h])
        ends = [links.arrival() for _ in range(5)]
        for off in OFFSETS:
            zz = turn(z, off)
            for s in range(2):
                for sec in range(2):
                    value = prods[h][chains[3, lax.rem(sec + core, 2) * Q + zz * 2 + s]].astype(BF16)
                    for half in range(2):
                        terms[h][half, zz * 2 + s, pl.ds(sec * 64, 64)] = value[half * 64 : half * 64 + 64]
            chunk = pl.ds(zz * 2, 2)
            links.send(terms[h].at[1 - core, chunk], xterms[h].at[chunk], sibling, batch, ends[min(off, N - off)])
        return ends

    for prod in prods:
        prod[NT] = jnp.zeros((TILE, TILE), F32)
    share0, share1 = share(0), share(1)
    step(share0)
    transpose(0)
    step(share1)
    transpose(1)
    weight_t[...] = weight[...].T
    chained.wait()
    for _ in range(2):
        step(share0)
        step(share1)
    step(share0)

    def sum_parts(h, slots, last):
        def fin(value):
            agg[h] = value.astype(BF16)

        def prep(p):
            for s in range(2):
                parts[h][p * 2 + s] = prods[h][chains[1, s * N + p]].astype(BF16)

        return scatter_ring(links, parts[h], prep, slots, last, y, xl, y_ways, near_x, fin)

    forward0, forward1 = forward(0), forward(1)
    step(forward0)
    drain(share0)
    drain(forward0)
    sum0 = sum_parts(0, fslots0, flast0)
    step(sum0)
    step(share1)
    step(forward1)
    drain(share1)
    drain(forward1)
    sum1 = sum_parts(1, fslots1, flast1)
    for _ in range(2):
        step(sum1)
        step(sum0)
    step(sum1)
    drain(sum0)

    pre = jnp.dot(agg[0], weight[pl.ds(0, TILE)], preferred_element_type=F32)
    drain(sum1)
    pre = pre + jnp.dot(agg[1], weight[pl.ds(TILE, TILE)], preferred_element_type=F32)
    gate = jax.nn.sigmoid(pre)
    gpre[...] = (gout[...].astype(F32) * gate * (1.0 + pre * (1.0 - gate))).astype(BF16)
    own = y * 2 + xl
    grads = []
    for h in range(2):
        gbufs[h][own] = jnp.dot(gpre[...], weight_t[:, pl.ds(h * TILE, TILE)], preferred_element_type=F32).astype(BF16)
        grads.append(gather_ring(links, gbufs[h], y, xl, y_ways, near_x))
        step(grads[h])

    act_out[...] = (pre * gate).astype(BF16)
    gpre_t = gpre[...].T
    rows = 2 * TILE // Q
    for h in range(2):
        value = jnp.dot(gpre_t, agg[h], preferred_element_type=F32).astype(BF16)
        for p in range(Q):
            wt[h, (p % N) * 2 + p // N] = value[p * rows : (p + 1) * rows]

    def weight_gradient():
        pair = links.send(wt.at[1 - core], wpair, sibling, links.batch(wpair))
        yield
        pair.wait_recv()
        for q in range(Q):
            wt[core, q] = (wt[core, q].astype(F32) + wpair[q].astype(F32)).astype(BF16)

        def fin(value):
            wgather[place] = value.astype(BF16)

        ring = scatter_ring(links, wt.at[core], lambda p: None, wslots, wlast, y, xl, y_ways, near_x, fin)
        for _ in range(3):
            step(ring)
            yield
        drain(ring)
        ring = gather_ring(links, wgather, z, xh, z_ways, far_x)
        for _ in range(3):
            step(ring)
            yield
        drain(ring)
        value = wgather[0].astype(F32)
        for q in range(1, Q):
            value = value + wgather[q].astype(F32)
        wsum[core] = value
        half = wsum.at[core]
        pair = links.send(half, half, sibling, links.batch(half))
        yield
        pair.wait_recv()
        for h in range(2):
            gw_out[:, pl.ds(h * TILE, TILE)] = wsum[h]
        yield

    wgrad = weight_gradient()
    step(wgrad)
    step(grads[0])
    step(wgrad)
    step(grads[1])
    step(grads[0])
    step(grads[1])
    step(wgrad)
    step(grads[0])
    backward0, backward1 = backward(0), backward(1)
    drain(backward0)

    def sum_terms(h, ends, slots, last):
        order = iter(OFFSETS)

        def prep(p):
            off = next(order)
            if off <= HALF:
                await_bytes(xterms[h].at[pl.ds(0, 2 if off in (0, HALF) else 4)], ends[off])
            for s in range(2):
                value = terms[h][core, p * 2 + s].astype(F32) + xterms[h][p * 2 + s].astype(F32)
                terms[h][core, p * 2 + s] = value.astype(BF16)

        def fin(value):
            for sec in range(2):
                gf_out[sec, :, pl.ds(h * TILE, TILE)] = value[sec * 64 : sec * 64 + 64]

        return scatter_ring(links, terms[h].at[core], prep, slots, last, z, xh, z_ways, far_x, fin)

    out0 = sum_terms(0, pair_terms(0), bslots0, blast0)
    step(out0)
    drain(grads[1])
    drain(backward1)
    step(wgrad, 2)
    out1 = sum_terms(1, pair_terms(1), bslots1, blast1)
    step(out0)
    step(out1)
    step(wgrad)
    step(out0)
    step(out1)
    step(wgrad)
    drain(out0)
    step(out1)
    step(wgrad)
    drain(out1)
    drain(wgrad)
    links.finish()


def store(*refs):
    copies = [pltpu.make_async_copy(refs[i], refs[3 + i], refs[6].at[i]) for i in range(3)]
    for copy in copies:
        copy.start()
    for copy in copies:
        copy.wait()


def shards(features, adjacency, tile_ids, tile_counts, weight, grad_out):
    block = (TILE, TILE)
    hbm = pl.BlockSpec(memory_space=pltpu.HBM)
    vmem = pl.BlockSpec(memory_space=pltpu.VMEM)
    rows = 2 * TILE // Q
    stripe, part = (rows, 2 * TILE), (rows, TILE)
    slots, last = (2, 5), (5,)
    activated, grad_weight, grad_features = pl.pallas_call(
        kernel,
        out_shape=(
            pltpu.VMEM((TILE, 2 * TILE), BF16),
            pltpu.VMEM(stripe, F32),
            pltpu.VMEM((2, 64, 2 * TILE), F32),
        ),
        in_specs=[hbm] * 6,
        out_specs=(vmem, vmem, vmem),
        scratch_shapes=[
            pltpu.VMEM((2,) + block, BF16),
            pltpu.VMEM((1, 2, SLOTS) + block, BF16),
            *[pltpu.VMEM((2 * TILE, 2 * TILE), BF16)] * 2,
            pltpu.VMEM((TILE, 2 * TILE), BF16),
            *[pltpu.VMEM((Q,) + block, BF16)] * 4,
            *[pltpu.VMEM((Q,) + block, BF16)] * 2,
            *[pltpu.VMEM((Q,) + block, BF16)] * 2,
            *[pltpu.VMEM((2, Q) + block, BF16)] * 2,
            *[pltpu.VMEM((Q,) + block, BF16)] * 2,
            pltpu.VMEM((NT,) + block, BF16),
            *[pltpu.VMEM((NT + 1,) + block, F32)] * 2,
            pltpu.VMEM((2,) + block, BF16),
            pltpu.VMEM((TILE, 2 * TILE), BF16),
            *[pltpu.VMEM(slots + block, BF16)] * 2,
            *[pltpu.VMEM(last + block, BF16)] * 2,
            *[pltpu.VMEM(slots + block, BF16)] * 2,
            *[pltpu.VMEM(last + block, BF16)] * 2,
            pltpu.VMEM((2, Q) + part, BF16),
            pltpu.VMEM((Q,) + part, BF16),
            pltpu.VMEM(slots + part, BF16),
            pltpu.VMEM(last + part, BF16),
            pltpu.VMEM((2,) + part, F32),
            pltpu.VMEM((Q,) + part, BF16),
            pltpu.SMEM((1, 2, SLOTS), jnp.int32),
            pltpu.SMEM((1, 2), jnp.int32),
            pltpu.VMEM((8, TILE), jnp.int32),
            pltpu.SMEM((8, TILE), jnp.int32),
            pltpu.SemaphoreType.DMA((8,)),
            pltpu.SemaphoreType.DMA((N_SEND,)),
            pltpu.SemaphoreType.DMA((N_RECV,)),
        ],
        compiler_params=pltpu.CompilerParams(
            collective_id=0, has_side_effects=True, vmem_limit_bytes=40 * 1024 * 1024
        ),
    )(*[pltpu.with_memory_space_constraint(x, pltpu.HBM) for x in (features, adjacency, tile_ids, tile_counts, weight, grad_out)])
    results = (activated, grad_weight, grad_features)
    activated, grad_weight, grad_features = pl.pallas_call(
        store,
        out_shape=[pltpu.HBM(x.shape, x.dtype) for x in results],
        in_specs=[vmem] * 3,
        out_specs=[hbm] * 3,
        scratch_shapes=[pltpu.SemaphoreType.DMA((3,))],
    )(*[pltpu.with_memory_space_constraint(x, pltpu.VMEM) for x in results])
    return activated, grad_weight.T, grad_features


def solution(mesh):
    return jax.shard_map(
        shards,
        mesh=mesh,
        in_specs=(
            P(("rows", "rep"), None),
            P("rows", "rep", None, None, None),
            P("rows", "rep", None),
            P("rows", "rep"),
            P(),
            P(("rows", "rep"), None),
        ),
        out_specs=(P(("rows", "rep"), None), P(None, "rep"), P("rep", "rows", None)),
        check_vma=False,
    )
```
